128 devices in a mesh: outer: 8 (over y, core), inner: 16 (over z, x).
Axes of the slice: x: 4, y: 4, z: 4, core: 2. Of those that a mesh axis runs over, the one named last changes fastest.
Arguments:
- points: bfloat16 [262144, 2048], P(('outer', 'inner')), may hold values from -6 to 6
- leaf_order: int32 [128, 2048], P(('outer', 'inner')), may hold values from 0 to 2047, each once within a row
- diag_blocks: bfloat16 [128, 2048, 2048], P(('outer', 'inner')), may hold values from -0.125 to 0.125
- leaf_basis: bfloat16 [128, 2048, 256], P(('outer', 'inner')), may hold values from -0.125 to 0.125
- leaf_nodes: bfloat16 [128, 2, 256, 256], P(('outer', 'inner')), may hold values from -1.5 to 1.5
- inner_nodes: bfloat16 [8, 15, 2, 256, 256], P('outer'), may hold values from -1.5 to 1.5
- outer_nodes: bfloat16 [6, 2, 256, 256], replicated, may hold values from -1.5 to 1.5
- root_coupling: bfloat16 [256, 256], replicated, may hold values from -1.5 to 1.5
- node_ranks: int32 [255], replicated, may hold values from 64 to 256
Outputs:
- product: bfloat16 [262144, 2048], P(('outer', 'inner'))
The draws below stay inside these ranges and needn't reach their ends.
Inputs may be any that keep to these rules, and one draw needn't show every extreme that they name: `leaf_order`: each row is a permutation of the positions 0 to 2047 within the leaf's block.
All inputs are finite; a program needn't handle non-finite values.
Results may differ from the reference program's by a relative error of at most 0.017.
Values may be sent and summed in bfloat16 or wider, within the bound.
No kernel may reach another device: no remote copies, remote signals or barrier semaphores. Data moves between devices by JAX's collectives and lax.ppermute only.
A program may use at most 256 MiB of HBM per device.

```python
import math
import jax
import jax.numpy as jnp
from jax import lax

LEAF = 2048
RANK = 256
VECS = 2048
LEAVES = 128
POINTS = 262144
NODES = 255
N_OUTER = 8
N_INNER = 16


off_weight = 0.3


transfer_scale = 0.85


coupling_scale = 1.0


def build_matrices(off_part, diag_values, scales, rank_width):
    rows = jnp.arange(rank_width, dtype=jnp.int32)
    identity = (rows[:, None] == rows[None, :]).astype(jnp.float32)
    matrix = off_part * (off_weight / math.sqrt(rank_width)) + identity * diag_values[..., :, None]
    return matrix * scales


def pair_scales():
    return jnp.array([transfer_scale, coupling_scale], dtype=jnp.float32).reshape(2, 1, 1)


def draw_leaf_nodes(key, part):
    key = jax.random.fold_in(key, 21)
    off_key, diag_key = jax.random.split(key)
    shape = (LEAVES, 2, RANK, RANK)
    off_part = jnp.clip(jax.random.normal(off_key, shape, jnp.float32), -4.0, 4.0)
    diag_values = jax.random.uniform(diag_key, shape[:-1], jnp.float32, 0.8, 1.2)
    return build_matrices(off_part, diag_values, pair_scales(), RANK).astype(jnp.bfloat16)


def draw_inner_nodes(key, part):
    key = jax.random.fold_in(key, 22)
    off_key, diag_key = jax.random.split(key)
    shape = (N_OUTER, N_INNER - 1, 2, RANK, RANK)
    off_part = jnp.clip(jax.random.normal(off_key, shape, jnp.float32), -4.0, 4.0)
    diag_values = jax.random.uniform(diag_key, shape[:-1], jnp.float32, 0.8, 1.2)
    return build_matrices(off_part, diag_values, pair_scales(), RANK).astype(jnp.bfloat16)


def draw_outer_nodes(key, part):
    key = jax.random.fold_in(key, 23)
    off_key, diag_key = jax.random.split(key)
    shape = (N_OUTER - 2, 2, RANK, RANK)
    off_part = jnp.clip(jax.random.normal(off_key, shape, jnp.float32), -4.0, 4.0)
    diag_values = jax.random.uniform(diag_key, shape[:-1], jnp.float32, 0.8, 1.2)
    return build_matrices(off_part, diag_values, pair_scales(), RANK).astype(jnp.bfloat16)


def draw_root_coupling(key, part):
    key = jax.random.fold_in(key, 24)
    off_key, diag_key = jax.random.split(key)
    shape = (RANK, RANK)
    off_part = jnp.clip(jax.random.normal(off_key, shape, jnp.float32), -4.0, 4.0)
    diag_values = jax.random.uniform(diag_key, shape[:-1], jnp.float32, 0.8, 1.2)
    return build_matrices(off_part, diag_values, coupling_scale, RANK).astype(jnp.bfloat16)


def draw_node_ranks(key, part):
    key = jax.random.fold_in(key, 11)
    drawn = jax.random.randint(key, (NODES,), 3 * RANK // 4, RANK + 1, dtype=jnp.int32)
    drawn = drawn.at[0].set(RANK)
    drawn = drawn.at[1].set(RANK // 4)
    return drawn


def shard_levels(key, extent, pieces, smallest, top_value):
    level = 1.0
    for position, parts in pieces:
        steps = jax.random.uniform(jax.random.fold_in(jax.random.fold_in(key, 6), position), (parts,), jnp.float32, smallest / len(pieces), top_value / len(pieces))
        level = level * jnp.repeat(jnp.exp(steps), extent[position] // parts).reshape((-1,) + (1,) * (len(extent) - 1 - position))
    return level


def gaussian(own_key, extent, deviation, limit, cuts=(), kind=jnp.bfloat16):
    level = shard_levels(own_key, extent, cuts, -0.22, 0.18) if cuts else 1.0
    entries = jax.random.normal(own_key, extent, jnp.float32) * deviation * level
    return jnp.minimum(jnp.maximum(entries, -limit), limit).astype(kind)


def setup_inputs(seed: int = 0) -> dict:
    keys = jax.random.split(jax.random.key(seed), 10)
    return {
        "points": gaussian(keys[0], (POINTS, VECS), 1.0, 6.0, ((0, 128),)),
        "leaf_order": jax.vmap(lambda own: jax.random.permutation(own, LEAF))(jax.random.split(keys[1], LEAVES)).reshape((LEAVES, LEAF)).astype(jnp.int32),
        "diag_blocks": gaussian(keys[2], (LEAVES, LEAF, LEAF), LEAF ** -0.5, 0.125, ((0, 128),)),
        "leaf_basis": gaussian(keys[3], (LEAVES, LEAF, RANK), LEAF ** -0.5, 0.125, ((0, 128),)),
        "leaf_nodes": draw_leaf_nodes(jax.random.fold_in(keys[9], 71), 0),
        "inner_nodes": draw_inner_nodes(jax.random.fold_in(keys[9], 71), 0),
        "outer_nodes": draw_outer_nodes(jax.random.fold_in(keys[9], 71), 0),
        "root_coupling": draw_root_coupling(jax.random.fold_in(keys[9], 71), 0),
        "node_ranks": draw_node_ranks(jax.random.fold_in(keys[9], 71), 0),
    }


def node_masks(node_ranks, height, leaf_count):
    node_count = leaf_count >> height
    heap_ids = node_count - 1 + jnp.arange(node_count, dtype=jnp.int32)
    limits = node_ranks[heap_ids]
    return (jnp.arange(RANK, dtype=jnp.int32)[None, :, None] < limits[:, None, None]).astype(jnp.float32)


def leaf_coef(pair):
    return jnp.dot(pair[0].T, pair[1], preferred_element_type=jnp.float32)


def leaf_value(items):
    near = jnp.dot(items[0], items[1], preferred_element_type=jnp.float32)
    return near + jnp.dot(items[2], items[3], preferred_element_type=jnp.float32)


def unpermute(positions, values):
    return jnp.zeros_like(values).at[positions].set(values)


def reference(points, leaf_order, diag_blocks, leaf_basis, leaf_nodes, inner_nodes, outer_nodes, root_coupling, node_ranks):
    count_outer = N_OUTER
    count_inner = N_INNER
    leaf_count = count_outer * count_inner
    depth_inner = count_inner.bit_length() - 1
    depth_outer = count_outer.bit_length() - 1
    depth_total = depth_inner + depth_outer
    blocks = points.reshape(leaf_count, LEAF, VECS)
    ordered = jnp.take_along_axis(blocks, leaf_order[:, :, None].astype(jnp.int32), axis=1)
    transfers = [leaf_nodes[:, 0]]
    couplings = [leaf_nodes[:, 1]]
    for height in range(1, depth_inner + 1):
        first_node = count_inner - (count_inner >> (height - 1))
        node_count = count_inner >> height
        section = inner_nodes[:, first_node:first_node + node_count].reshape(count_outer * node_count, 2, RANK, RANK)
        transfers.append(section[:, 0])
        couplings.append(section[:, 1])
    for segment in range(1, depth_outer):
        first_node = count_outer - (count_outer >> (segment - 1))
        node_count = count_outer >> segment
        section = outer_nodes[first_node:first_node + node_count]
        transfers.append(section[:, 0])
        couplings.append(section[:, 1])
    base = lax.map(leaf_coef, (leaf_basis, ordered))
    coefs = [(base * node_masks(node_ranks, 0, leaf_count)).astype(jnp.bfloat16)]
    for height in range(1, depth_total + 1):
        node_count = leaf_count >> height
        child_pairs = coefs[height - 1].reshape(node_count, 2, RANK, VECS).astype(jnp.float32)
        pair_transfer = transfers[height - 1].reshape(node_count, 2, RANK, RANK).astype(jnp.float32)
        upward = jnp.einsum('ncij,ncik->njk', pair_transfer, child_pairs)
        coefs.append((upward * node_masks(node_ranks, height, leaf_count)).astype(jnp.bfloat16))
    top = jnp.dot(root_coupling, coefs[depth_total][0], preferred_element_type=jnp.float32)
    far_coef = (top[None] * node_masks(node_ranks, depth_total, leaf_count)).astype(jnp.bfloat16)
    for height in reversed(range(depth_total)):
        node_count = leaf_count >> height
        sibling = coefs[height].reshape(node_count // 2, 2, RANK, VECS)[:, ::-1].reshape(node_count, RANK, VECS)
        parent = jnp.repeat(far_coef, 2, axis=0)
        summed = jnp.einsum('nij,njk->nik', couplings[height].astype(jnp.float32), sibling.astype(jnp.float32))
        summed = summed + jnp.einsum('nij,njk->nik', transfers[height].astype(jnp.float32), parent.astype(jnp.float32))
        far_coef = (summed * node_masks(node_ranks, height, leaf_count)).astype(jnp.bfloat16)
    values = lax.map(leaf_value, (diag_blocks, ordered, leaf_basis, far_coef)).astype(jnp.bfloat16)
    placed = jax.vmap(unpermute)(leaf_order.astype(jnp.int32), values)
    return placed.reshape(leaf_count * LEAF, VECS)
```

```python
import functools

import jax
import jax.numpy as jnp
from jax import lax
from jax.experimental import pallas as pl
from jax.experimental.pallas import tpu as pltpu
from jax.sharding import PartitionSpec as P

BF = jnp.bfloat16
F32 = jnp.float32
RING = 4
SMALL = 24 * 2**20


def nn(a, b):
    return jnp.dot(a, b, preferred_element_type=F32)


def nt(a, b):
    return lax.dot_general(a, b, (((1,), (1,)), ((), ())), preferred_element_type=F32)


def masked(value, rank):
    lane = lax.broadcasted_iota(jnp.int32, value.shape, 1)
    return jnp.where(lane < rank, value, 0.0).astype(BF)


def params(limit):
    return pltpu.CompilerParams(vmem_limit_bytes=limit)


def cost(flops, moved):
    return pl.CostEstimate(flops=flops, bytes_accessed=moved, transcendentals=0)


def sds(*shape):
    return jax.ShapeDtypeStruct(shape, BF)


def held(*shape):
    return pltpu.VMEM(shape, BF)


def pin(x, space=pltpu.VMEM):
    return pltpu.with_memory_space_constraint(x, space)


SMEM = pl.BlockSpec(memory_space=pltpu.SMEM)
VMEM = pl.BlockSpec(memory_space=pltpu.VMEM)
HBM = pl.BlockSpec(memory_space=pltpu.HBM)


def place():
    inner = lax.axis_index("inner")
    return inner & 3, inner >> 2, lax.axis_index("outer")


def call(kernel, name, out_shapes, args, flops=2**28, limit=8, scratch=(), specs=None):
    many = isinstance(out_shapes, tuple)
    return pl.pallas_call(
        kernel,
        out_shape=out_shapes,
        in_specs=specs or [SMEM] + [VMEM] * (len(args) - 1),
        out_specs=(VMEM,) * len(out_shapes) if many else VMEM,
        scratch_shapes=list(scratch),
        compiler_params=params(limit * 2**20),
        cost_estimate=cost(flops, 2**20),
        name=name,
    )(*args)


def shuffle_basis(order, basis, out, out_t, src, dst):
    rows = basis.shape[0]

    @pl.loop(0, rows // 64)
    def _(b):
        for r in range(4):
            for t in range(2):
                start = pl.multiple_of(b * 64 + r * 16, 16)
                x = basis[pl.ds(start, 16), t * 128 : (t + 1) * 128].astype(F32)
                base = (b * 64 + r * 16) * 3 + t
                src[pl.ds(base, 8, stride=3), :] = x[:8]
                src[pl.ds(base + 24, 8, stride=3), :] = x[8:]

    @pl.loop(0, rows // 64)
    def _(i):
        for j in range(64):
            to = order[0, i * 64 + j] * 3
            dst[pl.ds(to, 2), :] = src[pl.ds(i * 192 + j * 3, 2), :]

    @pl.loop(0, rows // 256)
    def _(b):
        for t in range(2):
            parts = []
            for r in range(32):
                base = (b * 256 + r * 8) * 3 + t
                parts.append(dst[pl.ds(base, 8, stride=3), :])
            x = jnp.concatenate(parts, axis=0)
            start = pl.multiple_of(b * 256, 256)
            out[pl.ds(start, 256), t * 128 : (t + 1) * 128] = x.astype(BF)
            out_t[t * 128 : (t + 1) * 128, pl.ds(start, 256)] = x.T.astype(BF)


def coef_block(shift, ranks, basis_t, x, transfer, coef, piece):
    ring, z, outer = place()
    cols = piece.shape[0]
    start = pl.multiple_of(lax.rem(ring + shift, RING) * cols, cols)
    rank = ranks[127 + outer * 16 + z * RING + ring]
    for j in range(0, cols, 256):
        c = masked(nn(basis_t[...], x[:, pl.ds(start + j, 256)]).T, rank)
        coef[pl.ds(start + j, 256), :] = c
        piece[j : j + 256] = nn(c, transfer[...]).astype(BF)


def front_kernel(
    order_hbm, ranks_hbm, basis_hbm, x_hbm, node_hbm,
    out, x, coef, p0, p1, p2, p3,
    order, ranks, basis, out_t, transfer, src, dst, sem,
):
    cols = p0.shape[0]
    ring = place()[0]

    def fetch(k):
        start = pl.multiple_of(lax.rem(ring + (2, 1, 3, 0)[k], RING) * cols, cols)
        part = pl.ds(start, cols)
        return pltpu.make_async_copy(x_hbm.at[:, part], x.at[:, part], sem.at[k])

    loads = [
        pltpu.make_async_copy(basis_hbm, basis, sem.at[4]),
        pltpu.make_async_copy(order_hbm, order, sem.at[5]),
        pltpu.make_async_copy(ranks_hbm, ranks, sem.at[6]),
        pltpu.make_async_copy(node_hbm.at[0], transfer, sem.at[7]),
    ]
    for load in loads:
        load.start()
    for k in range(RING):
        fetch(k).start()
    for load in loads:
        load.wait()
    shuffle_basis(order, basis, out, out_t, src, dst)
    for k, ref in enumerate((p2, p1, p3, p0)):
        fetch(k).wait()
        coef_block((2, 1, 3, 0)[k], ranks, out_t, x, transfer, coef, ref)


def front(order, ranks, basis, points, nodes):
    rows, width = basis.shape
    cols = points.shape[1]
    piece = held(cols // RING, width)
    return call(
        front_kernel,
        "front",
        (held(rows, width), held(rows, cols), held(cols, width)) + (piece,) * 4,
        [pin(a, pltpu.HBM) for a in (order, ranks, basis, points, nodes)],
        flops=2**31,
        limit=16,
        scratch=[
            pltpu.SMEM(order.shape, jnp.int32),
            pltpu.SMEM(ranks.shape, jnp.int32),
            pltpu.VMEM((rows, width), BF),
            pltpu.VMEM((width, rows), BF),
            pltpu.VMEM((width, width), BF),
            pltpu.VMEM((rows * 3, 128), F32),
            pltpu.VMEM((rows * 3, 128), F32),
            pltpu.SemaphoreType.DMA((8,)),
        ],
        specs=[HBM] * 5,
    )


PITCH = 9


def move_kernel(scatter, order, x, o, src, dst):
    rows = x.shape[0]

    for half in range(x.shape[1] // 1024):

        @pl.loop(0, rows // 32)
        def _(b):
            for r in range(2):
                base = (b * 32 + r * 16) * PITCH
                start = pl.multiple_of(b * 32 + r * 16, 16)
                for t in range(8):
                    at = half * 1024 + t * 128
                    v = x[pl.ds(start, 16), at : at + 128].astype(F32)
                    src[pl.ds(base + t, 8, stride=PITCH), :] = v[:8]
                    src[pl.ds(base + 8 * PITCH + t, 8, stride=PITCH), :] = v[8:]

        @pl.loop(0, rows // 64)
        def _(i):
            for j in range(64):
                far_at = order[0, i * 64 + j] * PITCH
                near_at = i * (64 * PITCH) + j * PITCH
                s, d = (near_at, far_at) if scatter else (far_at, near_at)
                dst[pl.ds(d, 8), :] = src[pl.ds(s, 8), :]

        @pl.loop(0, rows // 32)
        def _(b):
            for r in range(2):
                base = (b * 32 + r * 16) * PITCH
                start = pl.multiple_of(b * 32 + r * 16, 16)
                for t in range(8):
                    lo = dst[pl.ds(base + t, 8, stride=PITCH), :]
                    hi = dst[pl.ds(base + 8 * PITCH + t, 8, stride=PITCH), :]
                    at = half * 1024 + t * 128
                    v = jnp.concatenate([lo, hi], axis=0).astype(BF)
                    o[pl.ds(start, 16), at : at + 128] = v


def move_rows(scatter, order, x):
    rows, cols = x.shape
    return pl.pallas_call(
        functools.partial(move_kernel, scatter),
        out_shape=held(rows, cols),
        in_specs=[SMEM, VMEM],
        out_specs=VMEM,
        scratch_shapes=[pltpu.VMEM((rows * PITCH, 128), F32)] * 2,
        compiler_params=params(22 * 2**20),
        cost_estimate=cost(0, 18 * 2**20),
        name=f"move_{int(scatter)}",
    )(order, pin(x))


def near_kernel(first, d, x, out):
    size = out.shape[0]

    for j in range(0, x.shape[1], 256):
        out[:, j : j + 256] = nn(d[first : first + size], x[:, j : j + 256]).astype(BF)


def near_rows(piece, pieces, diag, ordered):
    rows, depth = diag.shape
    cols = ordered.shape[1]
    size = rows // pieces
    return pl.pallas_call(
        functools.partial(near_kernel, piece * size),
        out_shape=held(size, cols),
        in_specs=[VMEM] * 2,
        out_specs=VMEM,
        compiler_params=params(8 * 2**20),
        cost_estimate=cost(2 * size * depth * cols, 2**20),
        name=f"near_{piece}",
    )(pin(diag), pin(ordered))


def quad_up_kernel(ranks, u0, u1, u2, u3, inner, mid, p0, p1, p2, p3, leaf, top):
    x, z, outer = place()
    quad = outer * RING + z
    size = p0.shape[0]
    for s, ref in enumerate((u0, u1, u2, u3)):
        leaf[(x - s) & 3] = ref[...]
    for k in range(2):
        up = leaf[2 * k].astype(F32) + leaf[2 * k + 1].astype(F32)
        mid[k] = masked(up, ranks[63 + 2 * quad + k])
    up = nn(mid[0], inner[2 * z, 0]) + nn(mid[1], inner[2 * z + 1, 0])
    top[...] = masked(up, ranks[31 + quad])
    for t, ref in enumerate((p0, p1, p2, p3)):
        ref[...] = top[pl.ds(pl.multiple_of(((z + t) & 3) * size, size), size), :]


def quad_up(ranks, pieces, inner):
    cols, width = pieces[0].shape
    return call(
        quad_up_kernel,
        "quad_up",
        (held(2, cols, width),) + (held(cols // RING, width),) * 4,
        (ranks, *map(pin, pieces), pin(inner)),
        scratch=[pltpu.VMEM((4, cols, width), BF), pltpu.VMEM((cols, width), BF)],
    )


def group_up_kernel(ranks, q0, q1, q2, q3, inner, out2, out3, out4, lift):
    x, z, group = place()
    for t, ref in enumerate((q0, q1, q2, q3)):
        out2[(z - t) & 3] = ref[...]
    for k in range(2):
        up = nn(out2[2 * k], inner[8 + 2 * k, 0]) + nn(out2[2 * k + 1], inner[9 + 2 * k, 0])
        out3[k] = masked(up, ranks[15 + 2 * group + k])
    up = nn(out3[0], inner[12, 0]) + nn(out3[1], inner[13, 0])
    out4[...] = masked(up, ranks[7 + group])
    lift[...] = nn(out4[...], inner[14, 0])


def group_up(ranks, pieces, inner):
    part, width = pieces[0].shape
    return call(
        group_up_kernel,
        "group_up",
        (
            held(4, part, width),
            held(2, part, width),
            held(part, width),
            pltpu.VMEM((part, width), F32),
        ),
        (ranks, *map(pin, pieces), pin(inner)),
    )


def five_kernel(ranks, own, peer, out):
    out[...] = masked(own[...] + peer[...], ranks[3 + (place()[2] >> 1)])


def five_up(ranks, own, peer):
    return call(five_kernel, "five", held(*own.shape), (ranks, pin(own), pin(peer)))


def top_kernel(
    ranks, y0, y1, y2, y3, peer4, c2, c3, inner, outer, root, p0, p1, p2, p3, five, far2
):
    x, z, group = place()
    y = group >> 1
    half = y >> 1
    for s, ref in enumerate((y0, y1, y2, y3)):
        five[y ^ s] = ref[...]
    six = []
    for k in range(2):
        up = nn(five[2 * k], outer[2 * k, 0]) + nn(five[2 * k + 1], outer[2 * k + 1, 0])
        six.append(masked(up, ranks[1 + k]))
    up = nn(six[0], outer[4, 0]) + nn(six[1], outer[5, 0])
    seven = masked(up, ranks[0])
    far = masked(nt(seven, root[...]), ranks[0])
    sib = jnp.where(half == 0, six[1].astype(F32), six[0].astype(F32)).astype(BF)
    far = masked(nt(sib, outer[4 + half, 1]) + nt(far, outer[4 + half, 0]), ranks[1 + half])
    far = masked(nt(five[y ^ 1], outer[y, 1]) + nt(far, outer[y, 0]), ranks[3 + y])
    far = masked(nt(peer4[...], inner[14, 1]) + nt(far, inner[14, 0]), ranks[7 + group])
    for k in range(2):
        down = nt(c3[1 - k], inner[12 + k, 1]) + nt(far, inner[12 + k, 0])
        far3 = masked(down, ranks[15 + 2 * group + k])
        for i in (2 * k, 2 * k + 1):
            down = nt(c2[i ^ 1], inner[8 + i, 1]) + nt(far3, inner[8 + i, 0])
            far2[i] = masked(down, ranks[31 + 4 * group + i])
    for t, ref in enumerate((p0, p1, p2, p3)):
        ref[...] = far2[(z + t) & 3]


def top_sweep(ranks, fives, peer4, c2, c3, inner, outer, root):
    part, width = fives[0].shape
    return call(
        top_kernel,
        "top",
        (held(part, width),) * 4,
        (ranks, *map(pin, (*fives, peer4, c2, c3, inner, outer, root))),
        scratch=[pltpu.VMEM((4, part, width), BF)] * 2,
    )


def quad_down_kernel(ranks, f0, f1, f2, f3, mid, inner, p0, p1, p2, p3, far2, far1):
    x, z, outer = place()
    quad = outer * RING + z
    size = f0.shape[0]
    for t, ref in enumerate((f0, f1, f2, f3)):
        far2[pl.ds(pl.multiple_of(((z - t) & 3) * size, size), size), :] = ref[...]
    for k in range(2):
        down = nt(mid[1 - k], inner[2 * z + k, 1]) + nt(far2[...], inner[2 * z + k, 0])
        far1[k] = masked(down, ranks[63 + 2 * quad + k])
    for s, ref in enumerate((p0, p1, p2, p3)):
        ref[...] = far1[((x + s) & 3) >> 1]


def quad_down(ranks, fars, mid, inner):
    part, width = fars[0].shape
    cols = part * RING
    return call(
        quad_down_kernel,
        "quad_down",
        (held(cols, width),) * 4,
        (ranks, *map(pin, (*fars, mid, inner))),
        scratch=[pltpu.VMEM((cols, width), BF), pltpu.VMEM((2, cols, width), BF)],
    )


def tail_kernel(shift, ranks, basis, sibling, node, far1, *refs):
    nears = refs[:4]
    o_hbm, buf, sem = refs[-3:]
    x, z, outer = place()
    cols = far1.shape[0]
    size = nears[0].shape[0]
    at = pl.ds(pl.multiple_of(((x - shift) & 3) * cols, cols), cols)

    def put(k):
        return pltpu.make_async_copy(buf.at[k], o_hbm.at[pl.ds(k * size, size), at], sem.at[k])

    down = nt(sibling[at, :], node[1]) + nt(far1[...], node[0])
    far = masked(down, ranks[127 + outer * 16 + z * RING + x])
    for k, near in enumerate(nears):
        add = nt(basis[k * size : (k + 1) * size], far)
        buf[k] = (near[:, at].astype(F32) + add).astype(BF)
        put(k).start()
    for k in range(len(nears)):
        put(k).wait()


def add_far(shift, ranks, basis, sibling, node, far1, nears, sofar):
    rows, width = basis.shape
    cols = far1.shape[0]
    count = len(nears)
    args = [ranks] + [pin(a) for a in (basis, sibling, node, far1, *nears)]
    specs = [SMEM] + [VMEM] * (4 + count)
    alias = {}
    if sofar is not None:
        alias = {len(args): 0}
        args.append(sofar)
        specs.append(HBM)
    return pl.pallas_call(
        functools.partial(tail_kernel, shift),
        out_shape=sds(rows, nears[0].shape[1]),
        in_specs=specs,
        out_specs=HBM,
        input_output_aliases=alias,
        scratch_shapes=[
            pltpu.VMEM((count, rows // count, cols), BF),
            pltpu.SemaphoreType.DMA((count,)),
        ],
        compiler_params=params(8 * 2**20),
        cost_estimate=cost(2 * rows * width * cols, 3 * 2**20),
        name=f"tail_{shift}",
    )(*args)


def ring_x(block, shift):
    route = [(z * RING + x, z * RING + (x + shift) % RING) for z in range(RING) for x in range(RING)]
    return lax.ppermute(block, "inner", route)


def ring_z(block, shift):
    route = [(z * RING + x, (z + shift) % RING * RING + x) for z in range(RING) for x in range(RING)]
    return lax.ppermute(block, "inner", route)


def swap_inner(block, bits):
    return lax.ppermute(block, "inner", [(i, i ^ bits) for i in range(RING * RING)])


def swap_outer(block, bits):
    return lax.ppermute(block, "outer", [(o, o ^ bits) for o in range(2 * RING)])


def exchange(move, pieces, order=(2, 1, 3)):
    got = {0: pieces[0]}
    for s in order:
        got[s] = move(pieces[s], s)
    return [got[s] for s in range(RING)]


def body(
    points,
    leaf_order,
    diag_blocks,
    leaf_basis,
    leaf_nodes,
    inner_nodes,
    outer_nodes,
    root_coupling,
    node_ranks,
):
    ranks = node_ranks
    inner = inner_nodes[0]
    node = leaf_nodes[0]

    basis, x, coef, *pieces = front(leaf_order, ranks, leaf_basis[0], points, node)
    pieces = exchange(ring_x, pieces)
    ordered = move_rows(False, leaf_order, x)
    diag = move_rows(True, leaf_order, diag_blocks[0])
    *pieces, ordered, diag, coef = lax.optimization_barrier((*pieces, ordered, diag, coef))

    mid, *parts = quad_up(ranks, pieces, inner)
    coef, *parts = lax.optimization_barrier((coef, *parts))
    parts = exchange(ring_z, parts)
    sibling = swap_inner(coef, 1)
    nears = [near_rows(0, 4, diag, ordered)]
    *parts, nears[0] = lax.optimization_barrier((*parts, nears[0]))
    c2, c3, c4, lift = group_up(ranks, parts, inner)
    peer4 = swap_outer(c4, 1)
    five = five_up(ranks, lift, swap_outer(lift, 1))
    fives = [five] + [swap_outer(five, 2 * s) for s in (1, 2, 3)]
    nears.append(near_rows(1, 4, diag, ordered))
    *fives, nears[1] = lax.optimization_barrier((*fives, nears[1]))
    parts = top_sweep(ranks, fives, peer4, c2, c3, inner, outer_nodes, root_coupling)
    parts = exchange(ring_z, parts)
    nears.append(near_rows(2, 4, diag, ordered))
    *parts, nears[2] = lax.optimization_barrier((*parts, nears[2]))
    fars = quad_down(ranks, parts, mid, inner)
    fars = exchange(ring_x, fars)
    nears.append(near_rows(3, 4, diag, ordered))
    out = None
    for s in (0, 1, 3, 2):
        out = add_far(s, ranks, basis, sibling, node, fars[s], nears, out)
    return out


def solution(mesh):
    in_specs = (
        P(("outer", "inner"), None),
        P(("outer", "inner"), None),
        P(("outer", "inner"), None, None),
        P(("outer", "inner"), None, None),
        P(("outer", "inner"), None, None, None),
        P("outer", None, None, None, None),
        P(),
        P(),
        P(),
    )
    out_specs = P(("outer", "inner"), None)
    return jax.shard_map(body, mesh=mesh, in_specs=in_specs, out_specs=out_specs, check_vma=False)
```

```python
import functools

import jax
import jax.numpy as jnp
from jax import lax
from jax.experimental import pallas as pl
from jax.experimental.pallas import tpu as pltpu
from jax.sharding import PartitionSpec as P

BF = jnp.bfloat16
F32 = jnp.float32
RING = 4
SMALL = 24 * 2**20


def nn(a, b):
    return jnp.dot(a, b, preferred_element_type=F32)


def nt(a, b):
    return lax.dot_general(a, b, (((1,), (1,)), ((), ())), preferred_element_type=F32)


def masked(value, rank):
    lane = lax.broadcasted_iota(jnp.int32, value.shape, 1)
    return jnp.where(lane < rank, value, 0.0).astype(BF)


def params(limit):
    return pltpu.CompilerParams(vmem_limit_bytes=limit)


def cost(flops, moved):
    return pl.CostEstimate(flops=flops, bytes_accessed=moved, transcendentals=0)


def sds(*shape):
    return jax.ShapeDtypeStruct(shape, BF)


def held(*shape):
    return pltpu.VMEM(shape, BF)


def pin(x, space=pltpu.VMEM):
    return pltpu.with_memory_space_constraint(x, space)


SMEM = pl.BlockSpec(memory_space=pltpu.SMEM)
VMEM = pl.BlockSpec(memory_space=pltpu.VMEM)
HBM = pl.BlockSpec(memory_space=pltpu.HBM)


def place():
    inner = lax.axis_index("inner")
    return inner & 3, inner >> 2, lax.axis_index("outer")


def call(kernel, name, out_shapes, args, flops=2**28, limit=8, scratch=(), specs=None):
    many = isinstance(out_shapes, tuple)
    return pl.pallas_call(
        kernel,
        out_shape=out_shapes,
        in_specs=specs or [SMEM] + [VMEM] * (len(args) - 1),
        out_specs=(VMEM,) * len(out_shapes) if many else VMEM,
        scratch_shapes=list(scratch),
        compiler_params=params(limit * 2**20),
        cost_estimate=cost(flops, 2**20),
        name=name,
    )(*args)


def shuffle_basis(order, basis, out, out_t, src, dst):
    rows = basis.shape[0]

    @pl.loop(0, rows // 64)
    def _(b):
        for r in range(4):
            for t in range(2):
                start = pl.multiple_of(b * 64 + r * 16, 16)
                x = basis[pl.ds(start, 16), t * 128 : (t + 1) * 128].astype(F32)
                base = (b * 64 + r * 16) * 3 + t
                src[pl.ds(base, 8, stride=3), :] = x[:8]
                src[pl.ds(base + 24, 8, stride=3), :] = x[8:]

    @pl.loop(0, rows // 64)
    def _(i):
        for j in range(64):
            to = order[0, i * 64 + j] * 3
            dst[pl.ds(to, 2), :] = src[pl.ds(i * 192 + j * 3, 2), :]

    @pl.loop(0, rows // 256)
    def _(b):
        for t in range(2):
            parts = []
            for r in range(32):
                base = (b * 256 + r * 8) * 3 + t
                parts.append(dst[pl.ds(base, 8, stride=3), :])
            x = jnp.concatenate(parts, axis=0)
            start = pl.multiple_of(b * 256, 256)
            out[pl.ds(start, 256), t * 128 : (t + 1) * 128] = x.astype(BF)
            out_t[t * 128 : (t + 1) * 128, pl.ds(start, 256)] = x.T.astype(BF)


def coef_block(shift, ranks, basis_t, x, transfer, coef, piece):
    ring, z, outer = place()
    cols = piece.shape[0]
    start = pl.multiple_of(lax.rem(ring + shift, RING) * cols, cols)
    rank = ranks[127 + outer * 16 + z * RING + ring]
    c = masked(nn(basis_t[...], x[:, pl.ds(start, cols)]).T, rank)
    coef[pl.ds(start, cols), :] = c
    piece[...] = nn(c, transfer[...]).astype(BF)


def front_kernel(
    order_hbm, ranks_hbm, basis_hbm, x_hbm, node_hbm,
    out, x, coef, p0, p1, p2, p3,
    order, ranks, basis, out_t, transfer, src, dst, sem,
):
    cols = p0.shape[0]
    ring = place()[0]

    def fetch(k):
        start = pl.multiple_of(lax.rem(ring + (2, 1, 3, 0)[k], RING) * cols, cols)
        part = pl.ds(start, cols)
        return pltpu.make_async_copy(x_hbm.at[:, part], x.at[:, part], sem.at[k])

    loads = [
        pltpu.make_async_copy(basis_hbm, basis, sem.at[4]),
        pltpu.make_async_copy(order_hbm, order, sem.at[5]),
        pltpu.make_async_copy(ranks_hbm, ranks, sem.at[6]),
        pltpu.make_async_copy(node_hbm.at[0], transfer, sem.at[7]),
    ]
    for load in loads:
        load.start()
    for k in range(RING):
        fetch(k).start()
    for load in loads:
        load.wait()
    shuffle_basis(order, basis, out, out_t, src, dst)
    for k, ref in enumerate((p2, p1, p3, p0)):
        fetch(k).wait()
        coef_block((2, 1, 3, 0)[k], ranks, out_t, x, transfer, coef, ref)


def front(order, ranks, basis, points, nodes):
    rows, width = basis.shape
    cols = points.shape[1]
    piece = held(cols // RING, width)
    return call(
        front_kernel,
        "front",
        (held(rows, width), held(rows, cols), held(cols, width)) + (piece,) * 4,
        [pin(a, pltpu.HBM) for a in (order, ranks, basis, points, nodes)],
        flops=2**31,
        limit=16,
        scratch=[
            pltpu.SMEM(order.shape, jnp.int32),
            pltpu.SMEM(ranks.shape, jnp.int32),
            pltpu.VMEM((rows, width), BF),
            pltpu.VMEM((width, rows), BF),
            pltpu.VMEM((width, width), BF),
            pltpu.VMEM((rows * 3, 128), F32),
            pltpu.VMEM((rows * 3, 128), F32),
            pltpu.SemaphoreType.DMA((8,)),
        ],
        specs=[HBM] * 5,
    )


PITCH = 17


def move_rows(scatter, order, x, src, dst):
    rows = x.shape[0]
    tiles = x.shape[1] // 128

    @pl.loop(0, rows // 32)
    def _(b):
        for r in range(2):
            base = (b * 32 + r * 16) * PITCH
            start = pl.multiple_of(b * 32 + r * 16, 16)
            for t in range(tiles):
                v = x[pl.ds(start, 16), t * 128 : (t + 1) * 128].astype(F32)
                src[pl.ds(base + t, 8, stride=PITCH), :] = v[:8]
                src[pl.ds(base + 8 * PITCH + t, 8, stride=PITCH), :] = v[8:]

    @pl.loop(0, rows // 64)
    def _(i):
        for j in range(64):
            far_at = order[0, i * 64 + j]
            near_at = i * (64 * PITCH) + j * PITCH
            s, d = (near_at, far_at) if scatter else (far_at, near_at)
            for h in range(0, tiles, 8):
                dst[pl.ds(d + h, 8), :] = src[pl.ds(s + h, 8), :]

    @pl.loop(0, rows // 32)
    def _(b):
        for r in range(2):
            base = (b * 32 + r * 16) * PITCH
            start = pl.multiple_of(b * 32 + r * 16, 16)
            for t in range(tiles):
                lo = dst[pl.ds(base + t, 8, stride=PITCH), :]
                hi = dst[pl.ds(base + 8 * PITCH + t, 8, stride=PITCH), :]
                v = jnp.concatenate([lo, hi], axis=0).astype(BF)
                x[pl.ds(start, 16), t * 128 : (t + 1) * 128] = v


def move_kernel(order, x_in, diag_hbm, x, diag, src, dst, scaled, row_at, sem):
    size = diag.shape[0] // 4
    loads = []
    for k in range(4):
        part = pl.ds(k * size, size)
        loads.append(pltpu.make_async_copy(diag_hbm.at[part], diag.at[part], sem.at[k]))
        loads[k].start()
    scaled[...] = order[...] * PITCH
    load = pltpu.make_async_copy(scaled, row_at, sem.at[4])
    load.start()
    load.wait()
    move_rows(False, row_at, x, src, dst)
    for load in loads:
        load.wait()
    move_rows(True, row_at, diag, src, dst)


def move_both(order, x, diag):
    rows, cols = x.shape
    return pl.pallas_call(
        move_kernel,
        out_shape=(held(rows, cols), held(rows, cols)),
        in_specs=[VMEM, VMEM, HBM],
        out_specs=(VMEM, VMEM),
        input_output_aliases={1: 0},
        scratch_shapes=[pltpu.VMEM((rows * PITCH, 128), F32)] * 2
        + [
            pltpu.VMEM(order.shape, jnp.int32),
            pltpu.SMEM(order.shape, jnp.int32),
            pltpu.SemaphoreType.DMA((5,)),
        ],
        compiler_params=params(37 * 2**20),
        cost_estimate=cost(0, 40 * 2**20),
        name="move",
    )(pin(order), pin(x), pin(diag, pltpu.HBM))


def near_kernel(first, d, x, out):
    size = out.shape[0]

    for j in range(0, x.shape[1], 256):
        out[:, j : j + 256] = nn(d[first : first + size], x[:, j : j + 256]).astype(BF)


def near_rows(first, size, diag, ordered):
    rows, depth = diag.shape
    cols = ordered.shape[1]
    return pl.pallas_call(
        functools.partial(near_kernel, first),
        out_shape=held(size, cols),
        in_specs=[VMEM] * 2,
        out_specs=VMEM,
        compiler_params=params(8 * 2**20),
        cost_estimate=cost(2 * size * depth * cols, 2**20),
        name=f"near_{first}",
    )(pin(diag), pin(ordered))


def quad_up_kernel(ranks, u0, u1, u2, u3, inner, mid, p0, p1, p2, p3, leaf, top):
    x, z, outer = place()
    quad = outer * RING + z
    size = p0.shape[0]
    for s, ref in enumerate((u0, u1, u2, u3)):
        leaf[(x - s) & 3] = ref[...]
    for k in range(2):
        up = leaf[2 * k].astype(F32) + leaf[2 * k + 1].astype(F32)
        mid[k] = masked(up, ranks[63 + 2 * quad + k])
    up = nn(mid[0], inner[2 * z, 0]) + nn(mid[1], inner[2 * z + 1, 0])
    top[...] = masked(up, ranks[31 + quad])
    for t, ref in enumerate((p0, p1, p2, p3)):
        ref[...] = top[pl.ds(pl.multiple_of(((z + t) & 3) * size, size), size), :]


def quad_up(ranks, pieces, inner):
    cols, width = pieces[0].shape
    return call(
        quad_up_kernel,
        "quad_up",
        (held(2, cols, width),) + (held(cols // RING, width),) * 4,
        (ranks, *map(pin, pieces), pin(inner)),
        scratch=[pltpu.VMEM((4, cols, width), BF), pltpu.VMEM((cols, width), BF)],
    )


def group_up_kernel(ranks, q0, q1, q2, q3, inner, out2, out3, lift):
    x, z, group = place()
    for t, ref in enumerate((q0, q1, q2, q3)):
        out2[(z - t) & 3] = ref[...]
    for k in range(2):
        up = nn(out2[2 * k], inner[8 + 2 * k, 0]) + nn(out2[2 * k + 1], inner[9 + 2 * k, 0])
        out3[k] = masked(up, ranks[15 + 2 * group + k])
    up = nn(out3[0], inner[12, 0]) + nn(out3[1], inner[13, 0])
    four = masked(up, ranks[7 + group])
    lift[0] = four.astype(F32)
    lift[1] = nn(four, inner[14, 0])


def group_up(ranks, pieces, inner):
    part, width = pieces[0].shape
    return call(
        group_up_kernel,
        "group_up",
        (
            held(4, part, width),
            held(2, part, width),
            pltpu.VMEM((2, part, width), F32),
        ),
        (ranks, *map(pin, pieces), pin(inner)),
    )


def five_kernel(ranks, own, peer, out):
    out[...] = masked(own[1] + peer[1], ranks[3 + (place()[2] >> 1)])


def five_up(ranks, own, peer):
    return call(five_kernel, "five", held(*own.shape[1:]), (ranks, pin(own), pin(peer)))


def top_kernel(
    ranks, y0, y1, y2, y3, peer4, c2, c3, inner, outer, root, p0, p1, p2, p3, five, far2
):
    x, z, group = place()
    y = group >> 1
    half = y >> 1
    for s, ref in enumerate((y0, y1, y2, y3)):
        five[y ^ s] = ref[...]
    six = []
    for k in range(2):
        up = nn(five[2 * k], outer[2 * k, 0]) + nn(five[2 * k + 1], outer[2 * k + 1, 0])
        six.append(masked(up, ranks[1 + k]))
    up = nn(six[0], outer[4, 0]) + nn(six[1], outer[5, 0])
    seven = masked(up, ranks[0])
    far = masked(nt(seven, root[...]), ranks[0])
    sib = jnp.where(half == 0, six[1].astype(F32), six[0].astype(F32)).astype(BF)
    far = masked(nt(sib, outer[4 + half, 1]) + nt(far, outer[4 + half, 0]), ranks[1 + half])
    far = masked(nt(five[y ^ 1], outer[y, 1]) + nt(far, outer[y, 0]), ranks[3 + y])
    far = masked(nt(peer4[0].astype(BF), inner[14, 1]) + nt(far, inner[14, 0]), ranks[7 + group])
    for k in range(2):
        down = nt(c3[1 - k], inner[12 + k, 1]) + nt(far, inner[12 + k, 0])
        far3 = masked(down, ranks[15 + 2 * group + k])
        for i in (2 * k, 2 * k + 1):
            down = nt(c2[i ^ 1], inner[8 + i, 1]) + nt(far3, inner[8 + i, 0])
            far2[i] = masked(down, ranks[31 + 4 * group + i])
    for t, ref in enumerate((p0, p1, p2, p3)):
        ref[...] = far2[(z + t) & 3]


def top_sweep(ranks, fives, peer4, c2, c3, inner, outer, root):
    part, width = fives[0].shape
    return call(
        top_kernel,
        "top",
        (held(part, width),) * 4,
        (ranks, *map(pin, (*fives, peer4, c2, c3, inner, outer, root))),
        scratch=[pltpu.VMEM((4, part, width), BF)] * 2,
    )


def quad_down_kernel(ranks, f0, f1, f2, f3, mid, inner, p0, p1, p2, p3, far2, far1):
    x, z, outer = place()
    quad = outer * RING + z
    size = f0.shape[0]
    for t, ref in enumerate((f0, f1, f2, f3)):
        far2[pl.ds(pl.multiple_of(((z - t) & 3) * size, size), size), :] = ref[...]
    for k in range(2):
        down = nt(mid[1 - k], inner[2 * z + k, 1]) + nt(far2[...], inner[2 * z + k, 0])
        far1[k] = masked(down, ranks[63 + 2 * quad + k])
    for s, ref in enumerate((p0, p1, p2, p3)):
        ref[...] = far1[((x + s) & 3) >> 1]


def quad_down(ranks, fars, mid, inner):
    part, width = fars[0].shape
    cols = part * RING
    return call(
        quad_down_kernel,
        "quad_down",
        (held(cols, width),) * 4,
        (ranks, *map(pin, (*fars, mid, inner))),
        scratch=[pltpu.VMEM((cols, width), BF), pltpu.VMEM((2, cols, width), BF)],
    )


TAIL = 256


def tail_kernel(shifts, starts, ranks, basis, sibling, node, *refs):
    fars = refs[: len(shifts)]
    nears = refs[len(shifts) : len(shifts) + len(starts)]
    o_hbm, buf, sem = refs[-3:]
    x, z, outer = place()
    cols = fars[0].shape[0]
    rank = ranks[127 + outer * 16 + z * RING + x]
    copies = []
    for i, (shift, far1) in enumerate(zip(shifts, fars)):
        at = pl.ds(pl.multiple_of(((x - shift) & 3) * cols, cols), cols)
        down = nt(sibling[at, :], node[1]) + nt(far1[...], node[0])
        far = masked(down, rank)
        for first, near in zip(starts, nears):
            for r in range(0, near.shape[0], TAIL):
                row = first + r
                add = nt(basis[row : row + TAIL], far)
                buf[i, row : row + TAIL] = (near[r : r + TAIL, at].astype(F32) + add).astype(BF)
                copy = pltpu.make_async_copy(
                    buf.at[i, pl.ds(row, TAIL)], o_hbm.at[pl.ds(row, TAIL), at], sem.at[len(copies)]
                )
                copy.start()
                copies.append(copy)
    for copy in copies:
        copy.wait()


def add_far(shifts, starts, ranks, basis, sibling, node, fars, nears, sofar):
    rows, width = basis.shape
    cols = fars[0].shape[0]
    args = [ranks] + [pin(a) for a in (basis, sibling, node, *fars, *nears)]
    specs = [SMEM] + [VMEM] * (len(args) - 1)
    alias = {}
    if sofar is not None:
        alias = {len(args): 0}
        args.append(sofar)
        specs.append(HBM)
    return pl.pallas_call(
        functools.partial(tail_kernel, shifts, starts),
        out_shape=sds(rows, nears[0].shape[1]),
        in_specs=specs,
        out_specs=HBM,
        input_output_aliases=alias,
        scratch_shapes=[
            pltpu.VMEM((len(shifts), rows, cols), BF),
            pltpu.SemaphoreType.DMA((len(shifts) * rows // TAIL,)),
        ],
        compiler_params=params(12 * 2**20),
        cost_estimate=cost(2 * rows * width * cols, 3 * 2**20),
        name="tail_" + "".join(map(str, shifts)),
    )(*args)


def ring_x(block, shift):
    route = [(z * RING + x, z * RING + (x + shift) % RING) for z in range(RING) for x in range(RING)]
    return lax.ppermute(block, "inner", route)


def ring_z(block, shift):
    route = [(z * RING + x, (z + shift) % RING * RING + x) for z in range(RING) for x in range(RING)]
    return lax.ppermute(block, "inner", route)


def swap_inner(block, bits):
    return lax.ppermute(block, "inner", [(i, i ^ bits) for i in range(RING * RING)])


def swap_outer(block, bits):
    return lax.ppermute(block, "outer", [(o, o ^ bits) for o in range(2 * RING)])


def exchange(move, pieces, order=(2, 1, 3)):
    got = {0: pieces[0]}
    for s in order:
        got[s] = move(pieces[s], s)
    return [got[s] for s in range(RING)]


def body(
    points,
    leaf_order,
    diag_blocks,
    leaf_basis,
    leaf_nodes,
    inner_nodes,
    outer_nodes,
    root_coupling,
    node_ranks,
):
    ranks = node_ranks
    inner = inner_nodes[0]
    node = leaf_nodes[0]

    basis, x, coef, *pieces = front(leaf_order, ranks, leaf_basis[0], points, node)
    pieces = exchange(ring_x, pieces)
    ordered, diag = move_both(leaf_order, x, diag_blocks[0])
    *pieces, ordered, diag, coef = lax.optimization_barrier((*pieces, ordered, diag, coef))

    mid, *parts = quad_up(ranks, pieces, inner)
    coef, *parts = lax.optimization_barrier((coef, *parts))
    parts = exchange(ring_z, parts)
    sibling = swap_inner(coef, 1)
    starts = (0, 256, 768, 1024)
    nears = [near_rows(0, 256, diag, ordered)]
    *parts, nears[0] = lax.optimization_barrier((*parts, nears[0]))
    c2, c3, lift = group_up(ranks, parts, inner)
    peer = swap_outer(lift, 1)
    five = five_up(ranks, lift, peer)
    fives = [five] + [swap_outer(five, 2 * s) for s in (1, 2, 3)]
    nears.append(near_rows(256, 512, diag, ordered))
    *fives, nears[1] = lax.optimization_barrier((*fives, nears[1]))
    parts = top_sweep(ranks, fives, peer, c2, c3, inner, outer_nodes, root_coupling)
    parts = exchange(ring_z, parts)
    nears.append(near_rows(768, 256, diag, ordered))
    *parts, nears[2], sibling = lax.optimization_barrier((*parts, nears[2], sibling))
    fars = quad_down(ranks, parts, mid, inner)
    fars = exchange(ring_x, fars)
    nears.append(near_rows(1024, 1024, diag, ordered))
    add = functools.partial(add_far, starts=starts, ranks=ranks, basis=basis, sibling=sibling, node=node)
    out = add((0, 1, 3), fars=[fars[s] for s in (0, 1, 3)], nears=nears, sofar=None)
    return add((2,), fars=[fars[2]], nears=nears, sofar=out)


def solution(mesh):
    in_specs = (
        P(("outer", "inner"), None),
        P(("outer", "inner"), None),
        P(("outer", "inner"), None, None),
        P(("outer", "inner"), None, None),
        P(("outer", "inner"), None, None, None),
        P("outer", None, None, None, None),
        P(),
        P(),
        P(),
    )
    out_specs = P(("outer", "inner"), None)
    return jax.shard_map(body, mesh=mesh, in_specs=in_specs, out_specs=out_specs, check_vma=False)
```

```python
import functools

import jax
import jax.numpy as jnp
from jax import lax
from jax.experimental import pallas as pl
from jax.experimental.pallas import tpu as pltpu
from jax.sharding import PartitionSpec as P

BF = jnp.bfloat16
F32 = jnp.float32
RING = 4
SMALL = 24 * 2**20


def nn(a, b):
    return jnp.dot(a, b, preferred_element_type=F32)


def nt(a, b):
    return lax.dot_general(a, b, (((1,), (1,)), ((), ())), preferred_element_type=F32)


def masked(value, rank):
    lane = lax.broadcasted_iota(jnp.int32, value.shape, 1)
    return jnp.where(lane < rank, value, 0.0).astype(BF)


def params(limit):
    return pltpu.CompilerParams(vmem_limit_bytes=limit)


def cost(flops, moved):
    return pl.CostEstimate(flops=flops, bytes_accessed=moved, transcendentals=0)


def sds(*shape):
    return jax.ShapeDtypeStruct(shape, BF)


def held(*shape):
    return pltpu.VMEM(shape, BF)


def pin(x, space=pltpu.VMEM):
    return pltpu.with_memory_space_constraint(x, space)


SMEM = pl.BlockSpec(memory_space=pltpu.SMEM)
VMEM = pl.BlockSpec(memory_space=pltpu.VMEM)
HBM = pl.BlockSpec(memory_space=pltpu.HBM)


def place():
    inner = lax.axis_index("inner")
    return inner & 3, inner >> 2, lax.axis_index("outer")


def call(kernel, name, out_shapes, args, flops=2**28, limit=5, scratch=(), specs=None, alias={}):
    many = isinstance(out_shapes, tuple)
    return pl.pallas_call(
        kernel,
        out_shape=out_shapes,
        in_specs=specs or [SMEM] + [VMEM] * (len(args) - 1),
        out_specs=(VMEM,) * len(out_shapes) if many else VMEM,
        input_output_aliases=alias,
        scratch_shapes=list(scratch),
        compiler_params=params(limit * 2**20),
        cost_estimate=cost(flops, 2**20),
        name=name,
    )(*args)


def shuffle_basis(order, basis, out, out_t, src, dst):
    rows = basis.shape[0]

    @pl.loop(0, rows // 64)
    def _(b):
        for r in range(4):
            for t in range(2):
                start = pl.multiple_of(b * 64 + r * 16, 16)
                x = basis[pl.ds(start, 16), t * 128 : (t + 1) * 128].astype(F32)
                base = (b * 64 + r * 16) * 3 + t
                src[pl.ds(base, 8, stride=3), :] = x[:8]
                src[pl.ds(base + 24, 8, stride=3), :] = x[8:]

    @pl.loop(0, rows // 64)
    def _(i):
        for j in range(64):
            to = order[0, i * 64 + j] * 3
            dst[pl.ds(to, 2), :] = src[pl.ds(i * 192 + j * 3, 2), :]

    @pl.loop(0, rows // 256)
    def _(b):
        for t in range(2):
            parts = []
            for r in range(32):
                base = (b * 256 + r * 8) * 3 + t
                parts.append(dst[pl.ds(base, 8, stride=3), :])
            x = jnp.concatenate(parts, axis=0)
            start = pl.multiple_of(b * 256, 256)
            out[pl.ds(start, 256), t * 128 : (t + 1) * 128] = x.astype(BF)
            out_t[t * 128 : (t + 1) * 128, pl.ds(start, 256)] = x.T.astype(BF)


def coef_product(shift, basis_t, x):
    cols = x.shape[1] // RING
    start = pl.multiple_of(((place()[0] + shift) & 3) * cols, cols)
    return nn(basis_t[...], x[:, pl.ds(start, cols)])


def coef_finish(product, ranks, transfer, coef, piece):
    ring, z, outer = place()
    c = masked(product.T, ranks[127 + outer * 16 + z * RING + ring])
    coef[...] = c
    piece[...] = nn(c, transfer[...]).astype(BF)


def front_kernel(
    order_hbm, ranks_hbm, basis_hbm, x_hbm, node_hbm,
    out, out_t, x, coef, piece,
    order, ranks, basis, transfer, src, dst, sem,
):
    cols = piece.shape[0]
    ring = place()[0]

    def fetch(k):
        start = pl.multiple_of(lax.rem(ring + (2, 1, 3, 0)[k], RING) * cols, cols)
        part = pl.ds(start, cols)
        return pltpu.make_async_copy(x_hbm.at[:, part], x.at[:, part], sem.at[k])

    loads = [
        pltpu.make_async_copy(basis_hbm, basis, sem.at[4]),
        pltpu.make_async_copy(order_hbm, order, sem.at[5]),
        pltpu.make_async_copy(ranks_hbm, ranks, sem.at[6]),
        pltpu.make_async_copy(node_hbm.at[0], transfer, sem.at[7]),
    ]
    for load in loads:
        load.start()
    for load in loads:
        load.wait()
    for k in range(RING):
        fetch(k).start()
    shuffle_basis(order, basis, out, out_t, src, dst)
    fetch(0).wait()
    coef_finish(coef_product(2, out_t, x), ranks, transfer, coef, piece)
    for k in range(1, RING):
        fetch(k).wait()


def front(order, ranks, basis, points, nodes):
    rows, width = basis.shape
    cols = points.shape[1]
    return call(
        front_kernel,
        "front",
        (
            held(rows, width),
            held(width, rows),
            held(rows, cols),
            held(cols // RING, width),
            held(cols // RING, width),
        ),
        [pin(a, pltpu.HBM) for a in (order, ranks, basis, points, nodes)],
        flops=2**31,
        limit=13,
        scratch=[
            pltpu.SMEM(order.shape, jnp.int32),
            pltpu.SMEM(ranks.shape, jnp.int32),
            pltpu.VMEM((rows, width), BF),
            pltpu.VMEM((width, width), BF),
            pltpu.VMEM((rows * 3, 128), F32),
            pltpu.VMEM((rows * 3, 128), F32),
            pltpu.SemaphoreType.DMA((8,)),
        ],
        specs=[HBM] * 5,
    )


def coef_kernel(ranks, basis_t, x, node, c1, c3, p1, p3):
    product1 = coef_product(1, basis_t, x)
    product3 = coef_product(3, basis_t, x)
    coef_finish(product1, ranks, node.at[0], c1, p1)
    coef_finish(product3, ranks, node.at[0], c3, p3)


def coef_rest(ranks, basis_t, x, node):
    return call(
        coef_kernel,
        "coef",
        (held(x.shape[1] // RING, basis_t.shape[0]),) * 4,
        (ranks, *map(pin, (basis_t, x, node))),
        flops=2**30,
    )


PITCH = 17
GROUP = 64


def spread(value, first_row, first_tile, to):
    for r in range(0, value.shape[0], 8):
        for t in range(value.shape[1] // 128):
            at = (first_row + r) * PITCH + first_tile + t
            to[pl.ds(at, 8, stride=PITCH), :] = value[r : r + 8, t * 128 : (t + 1) * 128]


def gathered(first_row, rows, first_tile, tiles, of):
    columns = []
    for t in range(tiles):
        parts = []
        for r in range(0, rows, 8):
            at = (first_row + r) * PITCH + first_tile + t
            parts.append(of[pl.ds(at, 8, stride=PITCH), :])
        columns.append(jnp.concatenate(parts, axis=0))
    return jnp.concatenate(columns, axis=1)


def move_rows(row_at, x, src, dst):
    rows = x.shape[0]
    tiles = x.shape[1] // 128

    @pl.loop(0, rows // 32)
    def _(b):
        for r in range(0, 32, 16):
            start = pl.multiple_of(b * 32 + r, 16)
            for t in range(tiles):
                v = x[pl.ds(start, 16), t * 128 : (t + 1) * 128].astype(F32)
                spread(v, b * 32 + r, t, src)

    @pl.loop(0, rows // (2 * GROUP))
    def _(i):
        first = pl.multiple_of(i * (2 * GROUP), 2 * GROUP)
        for g in range(2):
            for j in range(GROUP):
                s = row_at[0, first + g * GROUP + j]
                for h in range(0, tiles, 8):
                    dst[g][pl.ds(j * PITCH + h, 8), :] = src[pl.ds(s + h, 8), :]
        for g in range(2):
            for r in range(0, GROUP, 16):
                for t in range(tiles):
                    v = gathered(r, 16, t, 1, dst[g]).astype(BF)
                    x[pl.ds(first + g * GROUP + r, 16), t * 128 : (t + 1) * 128] = v


def move_kernel(
    ranks, order, basis_t, node, c1, c2, c3, x_in, diag_hbm,
    coef, x, diag, piece, src,
    even, odd, scaled, row_at, sem,
):
    size = diag.shape[0] // 4
    loads = []
    for k in range(4):
        part = pl.ds(k * size, size)
        loads.append(pltpu.make_async_copy(diag_hbm.at[part], diag.at[part], sem.at[k]))
        loads[k].start()
    scaled[...] = order[...] * PITCH
    load = pltpu.make_async_copy(scaled, row_at, sem.at[4])
    load.start()
    cols = piece.shape[0]
    ring = place()[0]

    def rows_of(shift):
        return coef.at[pl.ds(pl.multiple_of(((ring + shift) & 3) * cols, cols), cols)]

    coef_finish(coef_product(0, basis_t, x), ranks, node.at[0], rows_of(0), piece)
    for shift, ref in ((1, c1), (2, c2), (3, c3)):
        rows_of(shift)[...] = ref[...]
    load.wait()
    move_rows(row_at, x, src, (even, odd))
    for load in loads:
        load.wait()


def move(ranks, order, basis_t, node, coefs, x, diag):
    rows, cols = x.shape
    width = basis_t.shape[0]
    return call(
        move_kernel,
        "move",
        (
            held(cols, width),
            held(rows, cols),
            held(rows, cols),
            held(cols // RING, width),
            pltpu.VMEM((rows * PITCH, 128), F32),
        ),
        (ranks, *map(pin, (order, basis_t, node, *coefs, x)), pin(diag, pltpu.HBM)),
        flops=2**33,
        limit=6,
        scratch=[
            pltpu.VMEM((GROUP * PITCH, 128), F32),
            pltpu.VMEM((GROUP * PITCH, 128), F32),
            pltpu.VMEM(order.shape, jnp.int32),
            pltpu.SMEM(order.shape, jnp.int32),
            pltpu.SemaphoreType.DMA((5,)),
        ],
        specs=[SMEM] + [VMEM] * 7 + [HBM],
        alias={7: 1},
    )


def near_kernel(first, size, order, d, x, near_in, out, even, odd, row_at, sem):
    block = even.shape[0] // PITCH
    load = pltpu.make_async_copy(order, row_at, sem)
    load.start()
    waiting = []

    def place_rows(count):
        for _ in range(min(count, len(waiting))):
            row, i, h, src = waiting.pop(0)
            to = row_at[0, row + i] * PITCH
            out[pl.ds(to + h, 8), :] = src[pl.ds(i * PITCH + h, 8), :]

    steps = x.shape[1] // 256
    for k, row in enumerate(range(first, first + size, block)):
        src = (even, odd)[k % 2]
        for j in range(steps):
            spread(nn(d[row : row + block], x[:, j * 256 : (j + 1) * 256]), 0, j * 2, src)
            if k == 0 and j == steps // 2 - 1:
                load.wait()
            place_rows(2 * block // steps)
            if j == steps // 2 - 1 or j == steps - 1:
                waiting += [(row, i, 8 * (2 * j // steps), src) for i in range(block)]
    place_rows(len(waiting))


def near_rows(first, size, order, diag, ordered, sofar):
    rows, depth = diag.shape
    cols = ordered.shape[1]
    block = min(size, 512)
    return call(
        functools.partial(near_kernel, first, size),
        f"near_{first}",
        pltpu.VMEM((rows * PITCH, 128), F32),
        tuple(map(pin, (order, diag, ordered, sofar))),
        flops=2 * size * depth * cols,
        limit=4 + block // 64,
        scratch=[pltpu.VMEM((block * PITCH, 128), F32)] * 2
        + [pltpu.SMEM(order.shape, jnp.int32), pltpu.SemaphoreType.DMA],
        specs=[VMEM] * 4,
        alias={3: 0},
    )


def quad_up_kernel(ranks, u0, u1, u2, u3, inner, mid, p0, p1, p2, p3, leaf, top):
    x, z, outer = place()
    quad = outer * RING + z
    size = p0.shape[0]
    for s, ref in enumerate((u0, u1, u2, u3)):
        leaf[(x - s) & 3] = ref[...]
    for k in range(2):
        up = leaf[2 * k].astype(F32) + leaf[2 * k + 1].astype(F32)
        mid[k] = masked(up, ranks[63 + 2 * quad + k])
    up = nn(mid[0], inner[2 * z, 0]) + nn(mid[1], inner[2 * z + 1, 0])
    top[...] = masked(up, ranks[31 + quad])
    for t, ref in enumerate((p0, p1, p2, p3)):
        ref[...] = top[pl.ds(pl.multiple_of(((z + t) & 3) * size, size), size), :]


def quad_up(ranks, pieces, inner):
    cols, width = pieces[0].shape
    return call(
        quad_up_kernel,
        "quad_up",
        (held(2, cols, width),) + (held(cols // RING, width),) * 4,
        (ranks, *map(pin, pieces), pin(inner)),
        scratch=[pltpu.VMEM((4, cols, width), BF), pltpu.VMEM((cols, width), BF)],
    )


def group_up_kernel(ranks, q0, q1, q2, q3, inner, out2, out3, lift):
    x, z, group = place()
    for t, ref in enumerate((q0, q1, q2, q3)):
        out2[(z - t) & 3] = ref[...]
    for k in range(2):
        up = nn(out2[2 * k], inner[8 + 2 * k, 0]) + nn(out2[2 * k + 1], inner[9 + 2 * k, 0])
        out3[k] = masked(up, ranks[15 + 2 * group + k])
    up = nn(out3[0], inner[12, 0]) + nn(out3[1], inner[13, 0])
    four = masked(up, ranks[7 + group])
    lift[0] = four.astype(F32)
    lift[1] = nn(four, inner[14, 0])


def group_up(ranks, pieces, inner):
    part, width = pieces[0].shape
    return call(
        group_up_kernel,
        "group_up",
        (
            held(4, part, width),
            held(2, part, width),
            pltpu.VMEM((2, part, width), F32),
        ),
        (ranks, *map(pin, pieces), pin(inner)),
    )


def five_kernel(ranks, own, peer, out):
    out[...] = masked(own[1] + peer[1], ranks[3 + (place()[2] >> 1)])


def five_up(ranks, own, peer):
    return call(five_kernel, "five", held(*own.shape[1:]), (ranks, pin(own), pin(peer)))


def top_kernel(
    ranks, y0, y1, y2, y3, peer4, c2, c3, inner, outer, root, p0, p1, p2, p3, five, far2
):
    x, z, group = place()
    y = group >> 1
    half = y >> 1
    for s, ref in enumerate((y0, y1, y2, y3)):
        five[y ^ s] = ref[...]
    six = []
    for k in range(2):
        up = nn(five[2 * k], outer[2 * k, 0]) + nn(five[2 * k + 1], outer[2 * k + 1, 0])
        six.append(masked(up, ranks[1 + k]))
    up = nn(six[0], outer[4, 0]) + nn(six[1], outer[5, 0])
    seven = masked(up, ranks[0])
    far = masked(nt(seven, root[...]), ranks[0])
    sib = jnp.where(half == 0, six[1].astype(F32), six[0].astype(F32)).astype(BF)
    far = masked(nt(sib, outer[4 + half, 1]) + nt(far, outer[4 + half, 0]), ranks[1 + half])
    far = masked(nt(five[y ^ 1], outer[y, 1]) + nt(far, outer[y, 0]), ranks[3 + y])
    far = masked(nt(peer4[0].astype(BF), inner[14, 1]) + nt(far, inner[14, 0]), ranks[7 + group])
    for k in range(2):
        down = nt(c3[1 - k], inner[12 + k, 1]) + nt(far, inner[12 + k, 0])
        far3 = masked(down, ranks[15 + 2 * group + k])
        for i in (2 * k, 2 * k + 1):
            down = nt(c2[i ^ 1], inner[8 + i, 1]) + nt(far3, inner[8 + i, 0])
            far2[i] = masked(down, ranks[31 + 4 * group + i])
    for t, ref in enumerate((p0, p1, p2, p3)):
        ref[...] = far2[(z + t) & 3]


def top_sweep(ranks, fives, peer4, c2, c3, inner, outer, root):
    part, width = fives[0].shape
    return call(
        top_kernel,
        "top",
        (held(part, width),) * 4,
        (ranks, *map(pin, (*fives, peer4, c2, c3, inner, outer, root))),
        scratch=[pltpu.VMEM((4, part, width), BF)] * 2,
    )


def quad_down_kernel(ranks, f0, f1, f2, f3, mid, inner, p0, p1, p2, p3, far2, far1):
    x, z, outer = place()
    quad = outer * RING + z
    size = f0.shape[0]
    for t, ref in enumerate((f0, f1, f2, f3)):
        far2[pl.ds(pl.multiple_of(((z - t) & 3) * size, size), size), :] = ref[...]
    for k in range(2):
        down = nt(mid[1 - k], inner[2 * z + k, 1]) + nt(far2[...], inner[2 * z + k, 0])
        far1[k] = masked(down, ranks[63 + 2 * quad + k])
    for s, ref in enumerate((p0, p1, p2, p3)):
        ref[...] = far1[((x + s) & 3) >> 1]


def quad_down(ranks, fars, mid, inner):
    part, width = fars[0].shape
    cols = part * RING
    return call(
        quad_down_kernel,
        "quad_down",
        (held(cols, width),) * 4,
        (ranks, *map(pin, (*fars, mid, inner))),
        scratch=[pltpu.VMEM((cols, width), BF), pltpu.VMEM((2, cols, width), BF)],
    )


TAIL = 512


def tail_kernel(shifts, ranks, basis, sibling, node, near, *refs):
    fars = refs[: len(shifts)]
    o_hbm, buf, sem = refs[-3:]
    x, z, outer = place()
    cols = fars[0].shape[0]
    rank = ranks[127 + outer * 16 + z * RING + x]
    copies = []
    for i, (shift, far1) in enumerate(zip(shifts, fars)):
        part = (x - shift) & 3
        at = pl.ds(pl.multiple_of(part * cols, cols), cols)
        tiles = cols // 128
        down = nt(sibling[at, :], node[1]) + nt(far1[...], node[0])
        far = masked(down, rank)
        for row in range(0, basis.shape[0], TAIL):
            add = nt(basis[row : row + TAIL], far)
            value = gathered(row, TAIL, part * tiles, tiles, near) + add
            buf[i, row : row + TAIL] = value.astype(BF)
            copy = pltpu.make_async_copy(
                buf.at[i, pl.ds(row, TAIL)], o_hbm.at[pl.ds(row, TAIL), at], sem.at[len(copies)]
            )
            copy.start()
            copies.append(copy)
    for copy in copies:
        copy.wait()


def add_far(shifts, ranks, basis, sibling, node, near, fars, sofar):
    rows, width = basis.shape
    cols = fars[0].shape[0]
    args = [ranks] + [pin(a) for a in (basis, sibling, node, near, *fars)]
    specs = [SMEM] + [VMEM] * (len(args) - 1)
    alias = {}
    if sofar is not None:
        alias = {len(args): 0}
        args.append(sofar)
        specs.append(HBM)
    return pl.pallas_call(
        functools.partial(tail_kernel, shifts),
        out_shape=sds(rows, cols * RING),
        in_specs=specs,
        out_specs=HBM,
        input_output_aliases=alias,
        scratch_shapes=[
            pltpu.VMEM((len(shifts), rows, cols), BF),
            pltpu.SemaphoreType.DMA((len(shifts) * rows // TAIL,)),
        ],
        compiler_params=params(14 * 2**20),
        cost_estimate=cost(2 * rows * width * cols, 3 * 2**20),
        name="tail_" + "".join(map(str, shifts)),
    )(*args)


def ring_x(block, shift):
    route = [(z * RING + x, z * RING + (x + shift) % RING) for z in range(RING) for x in range(RING)]
    return lax.ppermute(block, "inner", route)


def ring_z(block, shift):
    route = [(z * RING + x, (z + shift) % RING * RING + x) for z in range(RING) for x in range(RING)]
    return lax.ppermute(block, "inner", route)


def swap_inner(block, bits):
    return lax.ppermute(block, "inner", [(i, i ^ bits) for i in range(RING * RING)])


def swap_outer(block, bits):
    return lax.ppermute(block, "outer", [(o, o ^ bits) for o in range(2 * RING)])


def exchange(move, pieces, order=(2, 1, 3)):
    got = {0: pieces[0]}
    for s in order:
        got[s] = move(pieces[s], s)
    return [got[s] for s in range(RING)]


def body(
    points,
    leaf_order,
    diag_blocks,
    leaf_basis,
    leaf_nodes,
    inner_nodes,
    outer_nodes,
    root_coupling,
    node_ranks,
):
    ranks = node_ranks
    inner = inner_nodes[0]
    node = leaf_nodes[0]

    basis, basis_t, x, c2, piece = front(leaf_order, ranks, leaf_basis[0], points, node)
    c1, c3, *others = coef_rest(ranks, basis_t, x, node)
    sent = {2: ring_x(piece, 2), 1: ring_x(others[0], 1), 3: ring_x(others[1], 3)}
    coefs = (c1, c2, c3)
    coef, ordered, diag, own, near = move(ranks, leaf_order, basis_t, node, coefs, x, diag_blocks[0])
    near = near_rows(0, 256, leaf_order, diag, ordered, near)
    pieces = [own, sent[1], sent[2], sent[3]]
    *pieces, coef, near = lax.optimization_barrier((*pieces, coef, near))

    mid, *parts = quad_up(ranks, pieces, inner)
    coef, *parts = lax.optimization_barrier((coef, *parts))
    parts = exchange(ring_z, parts)
    sibling = swap_inner(coef, 1)
    near = near_rows(256, 256, leaf_order, diag, ordered, near)
    *parts, near = lax.optimization_barrier((*parts, near))
    c2, c3, lift = group_up(ranks, parts, inner)
    peer = swap_outer(lift, 1)
    five = five_up(ranks, lift, peer)
    fives = [five] + [swap_outer(five, 2 * s) for s in (1, 2, 3)]
    near = near_rows(512, 256, leaf_order, diag, ordered, near)
    *fives, near = lax.optimization_barrier((*fives, near))
    parts = top_sweep(ranks, fives, peer, c2, c3, inner, outer_nodes, root_coupling)
    parts = exchange(ring_z, parts)
    near = near_rows(768, 256, leaf_order, diag, ordered, near)
    *parts, near, sibling = lax.optimization_barrier((*parts, near, sibling))
    fars = quad_down(ranks, parts, mid, inner)
    fars = exchange(ring_x, fars)
    near = near_rows(1024, 1024, leaf_order, diag, ordered, near)
    add = functools.partial(add_far, ranks=ranks, basis=basis, sibling=sibling, node=node, near=near)
    return add((0, 1, 3, 2), fars=[fars[s] for s in (0, 1, 3, 2)], sofar=None)


def solution(mesh):
    in_specs = (
        P(("outer", "inner"), None),
        P(("outer", "inner"), None),
        P(("outer", "inner"), None, None),
        P(("outer", "inner"), None, None),
        P(("outer", "inner"), None, None, None),
        P("outer", None, None, None, None),
        P(),
        P(),
        P(),
    )
    out_specs = P(("outer", "inner"), None)
    return jax.shard_map(body, mesh=mesh, in_specs=in_specs, out_specs=out_specs, check_vma=False)
```

```python
import functools

import jax
import jax.numpy as jnp
from jax import lax
from jax.experimental import pallas as pl
from jax.experimental.pallas import tpu as pltpu
from jax.sharding import PartitionSpec as P

BF = jnp.bfloat16
F32 = jnp.float32
RING = 4
SMALL = 24 * 2**20


def nn(a, b):
    return jnp.dot(a, b, preferred_element_type=F32)


def nt(a, b):
    return lax.dot_general(a, b, (((1,), (1,)), ((), ())), preferred_element_type=F32)


def masked(value, limit):
    lane = lax.broadcasted_iota(jnp.int32, value.shape, 1)
    return jnp.where(lane < limit, value, 0.0).astype(BF)


def limit_of(table, heap_id):
    return table[pl.ds(heap_id, 1), :]


def params(limit):
    return pltpu.CompilerParams(vmem_limit_bytes=limit)


def cost(flops, moved):
    return pl.CostEstimate(flops=flops, bytes_accessed=moved, transcendentals=0)


def sds(*shape):
    return jax.ShapeDtypeStruct(shape, BF)


def held(*shape):
    return pltpu.VMEM(shape, BF)


def pin(x, space=pltpu.VMEM):
    return pltpu.with_memory_space_constraint(x, space)


VMEM = pl.BlockSpec(memory_space=pltpu.VMEM)
HBM = pl.BlockSpec(memory_space=pltpu.HBM)


def place():
    inner = lax.axis_index("inner")
    return inner & 3, inner >> 2, lax.axis_index("outer")


def call(kernel, name, out_shapes, args, flops=2**28, limit=5, scratch=(), specs=None, alias={}):
    many = isinstance(out_shapes, tuple)
    return pl.pallas_call(
        kernel,
        out_shape=out_shapes,
        in_specs=specs or [VMEM] * len(args),
        out_specs=(VMEM,) * len(out_shapes) if many else VMEM,
        input_output_aliases=alias,
        scratch_shapes=list(scratch),
        compiler_params=params(limit * 2**20),
        cost_estimate=cost(flops, 2**20),
        name=name,
    )(*args)


def shuffle_basis(order, basis, out, out_t, src, dst):
    rows = basis.shape[0]

    @pl.loop(0, rows // 64)
    def _(b):
        for r in range(4):
            for t in range(2):
                start = pl.multiple_of(b * 64 + r * 16, 16)
                x = basis[pl.ds(start, 16), t * 128 : (t + 1) * 128].astype(F32)
                base = (b * 64 + r * 16) * 3 + t
                src[pl.ds(base, 8, stride=3), :] = x[:8]
                src[pl.ds(base + 24, 8, stride=3), :] = x[8:]

    @pl.loop(0, rows // 64)
    def _(i):
        for j in range(64):
            to = order[0, i * 64 + j] * 3
            dst[pl.ds(to, 2), :] = src[pl.ds(i * 192 + j * 3, 2), :]

    @pl.loop(0, rows // 256)
    def _(b):
        for t in range(2):
            parts = []
            for r in range(32):
                base = (b * 256 + r * 8) * 3 + t
                parts.append(dst[pl.ds(base, 8, stride=3), :])
            x = jnp.concatenate(parts, axis=0)
            start = pl.multiple_of(b * 256, 256)
            out[pl.ds(start, 256), t * 128 : (t + 1) * 128] = x.astype(BF)
            out_t[t * 128 : (t + 1) * 128, pl.ds(start, 256)] = x.T.astype(BF)


def coef_product(shift, basis_t, x):
    cols = x.shape[1] // RING
    start = pl.multiple_of(((place()[0] + shift) & 3) * cols, cols)
    return nn(basis_t[...], x[:, pl.ds(start, cols)])


def coef_finish(product, limit, transfer, coef, piece):
    c = masked(product.T, limit[0:1])
    coef[...] = c
    piece[...] = nn(c, transfer[...]).astype(BF)


def front_kernel(
    order_hbm, ranks_hbm, basis_hbm, x_hbm, node_hbm,
    out, out_t, x, coef, piece, limit,
    order, ranks, basis, transfer, src, dst, sem,
):
    cols = piece.shape[0]
    ring, z, outer = place()

    def fetch(k):
        start = pl.multiple_of(lax.rem(ring + (2, 1, 3, 0)[k], RING) * cols, cols)
        part = pl.ds(start, cols)
        return pltpu.make_async_copy(x_hbm.at[:, part], x.at[:, part], sem.at[k])

    loads = [
        pltpu.make_async_copy(basis_hbm, basis, sem.at[4]),
        pltpu.make_async_copy(order_hbm, order, sem.at[5]),
        pltpu.make_async_copy(ranks_hbm, ranks, sem.at[6]),
        pltpu.make_async_copy(node_hbm.at[0], transfer, sem.at[7]),
    ]
    for load in loads:
        load.start()
    for load in loads:
        load.wait()
    for k in range(RING):
        fetch(k).start()
    limit[...] = jnp.full(limit.shape, ranks[127 + outer * 16 + z * RING + ring], jnp.int32)
    shuffle_basis(order, basis, out, out_t, src, dst)
    fetch(0).wait()
    coef_finish(coef_product(2, out_t, x), limit, transfer, coef, piece)
    for k in range(1, RING):
        fetch(k).wait()


def front(order, ranks, basis, points, nodes):
    rows, width = basis.shape
    cols = points.shape[1]
    return call(
        front_kernel,
        "front",
        (
            held(rows, width),
            held(width, rows),
            held(rows, cols),
            held(cols // RING, width),
            held(cols // RING, width),
            pltpu.VMEM((8, width), jnp.int32),
        ),
        [pin(a, pltpu.HBM) for a in (order, ranks, basis, points, nodes)],
        flops=2**31,
        limit=13,
        scratch=[
            pltpu.SMEM(order.shape, jnp.int32),
            pltpu.SMEM(ranks.shape, jnp.int32),
            pltpu.VMEM((rows, width), BF),
            pltpu.VMEM((width, width), BF),
            pltpu.VMEM((rows * 3, 128), F32),
            pltpu.VMEM((rows * 3, 128), F32),
            pltpu.SemaphoreType.DMA((8,)),
        ],
        specs=[HBM] * 5,
    )


def coef_kernel(limit, basis_t, x, node, c1, c3, p1, p3):
    product1 = coef_product(1, basis_t, x)
    product3 = coef_product(3, basis_t, x)
    coef_finish(product1, limit, node.at[0], c1, p1)
    coef_finish(product3, limit, node.at[0], c3, p3)


def coef_rest(limit, basis_t, x, node):
    return call(
        coef_kernel,
        "coef",
        (held(x.shape[1] // RING, basis_t.shape[0]),) * 4,
        tuple(map(pin, (limit, basis_t, x, node))),
        flops=2**30,
    )


PITCH = 17
GROUP = 64


def spread(value, first_row, first_tile, to):
    for r in range(0, value.shape[0], 8):
        for t in range(value.shape[1] // 128):
            at = (first_row + r) * PITCH + first_tile + t
            to[pl.ds(at, 8, stride=PITCH), :] = value[r : r + 8, t * 128 : (t + 1) * 128]


def gathered(first_row, rows, first_tile, tiles, of):
    columns = []
    for t in range(tiles):
        parts = []
        for r in range(0, rows, 8):
            at = (first_row + r) * PITCH + first_tile + t
            parts.append(of[pl.ds(at, 8, stride=PITCH), :])
        columns.append(jnp.concatenate(parts, axis=0))
    return jnp.concatenate(columns, axis=1)


def move_rows(row_at, x, src, dst):
    rows = x.shape[0]
    tiles = x.shape[1] // 128

    @pl.loop(0, rows // 32)
    def _(b):
        for r in range(0, 32, 16):
            start = pl.multiple_of(b * 32 + r, 16)
            for t in range(tiles):
                v = x[pl.ds(start, 16), t * 128 : (t + 1) * 128].astype(F32)
                spread(v, b * 32 + r, t, src)

    @pl.loop(0, rows // (2 * GROUP))
    def _(i):
        first = pl.multiple_of(i * (2 * GROUP), 2 * GROUP)
        for g in range(2):
            for j in range(GROUP):
                s = row_at[0, first + g * GROUP + j]
                for h in range(0, tiles, 8):
                    dst[g][pl.ds(j * PITCH + h, 8), :] = src[pl.ds(s + h, 8), :]
        for g in range(2):
            for r in range(0, GROUP, 16):
                for t in range(tiles):
                    v = gathered(r, 16, t, 1, dst[g]).astype(BF)
                    x[pl.ds(first + g * GROUP + r, 16), t * 128 : (t + 1) * 128] = v


def move_kernel(
    limit, order, basis_t, node, c1, c2, c3, x_in, diag_hbm, ranks_hbm,
    coef, x, diag, piece, src, table,
    even, odd, scaled, row_at, ranks, sem,
):
    size = diag.shape[0] // 4
    loads = []
    for k in range(4):
        part = pl.ds(k * size, size)
        loads.append(pltpu.make_async_copy(diag_hbm.at[part], diag.at[part], sem.at[k]))
        loads[k].start()
    scaled[...] = order[...] * PITCH
    load = pltpu.make_async_copy(scaled, row_at, sem.at[4])
    load.start()
    load_ranks = pltpu.make_async_copy(ranks_hbm, ranks, sem.at[5])
    load_ranks.start()
    cols = piece.shape[0]
    ring = place()[0]

    def rows_of(shift):
        return coef.at[pl.ds(pl.multiple_of(((ring + shift) & 3) * cols, cols), cols)]

    coef_finish(coef_product(0, basis_t, x), limit, node.at[0], rows_of(0), piece)
    for shift, ref in ((1, c1), (2, c2), (3, c3)):
        rows_of(shift)[...] = ref[...]
    load_ranks.wait()
    for node_id in range(ranks.shape[0]):
        table[node_id : node_id + 1] = jnp.full((1, table.shape[1]), ranks[node_id], jnp.int32)
    load.wait()
    move_rows(row_at, x, src, (even, odd))
    for load in loads:
        load.wait()


def move(limit, ranks, order, basis_t, node, coefs, x, diag):
    rows, cols = x.shape
    width = basis_t.shape[0]
    return call(
        move_kernel,
        "move",
        (
            held(cols, width),
            held(rows, cols),
            held(rows, cols),
            held(cols // RING, width),
            pltpu.VMEM((rows * PITCH, 128), F32),
            pltpu.VMEM((ranks.shape[0] + 1, width), jnp.int32),
        ),
        (
            *map(pin, (limit, order, basis_t, node, *coefs, x)),
            pin(diag, pltpu.HBM),
            pin(ranks, pltpu.HBM),
        ),
        flops=2**33,
        limit=6,
        scratch=[
            pltpu.VMEM((GROUP * PITCH, 128), F32),
            pltpu.VMEM((GROUP * PITCH, 128), F32),
            pltpu.VMEM(order.shape, jnp.int32),
            pltpu.SMEM(order.shape, jnp.int32),
            pltpu.SMEM(ranks.shape, jnp.int32),
            pltpu.SemaphoreType.DMA((6,)),
        ],
        specs=[VMEM] * 8 + [HBM] * 2,
        alias={7: 1},
    )


def near_kernel(first, size, order, d, x, near_in, out, even, odd, row_at, sem):
    block = even.shape[0] // PITCH
    load = pltpu.make_async_copy(order, row_at, sem)
    load.start()
    for k, row in enumerate(range(first, first + size, block)):
        src = (even, odd)[k % 2]
        for j in range(0, x.shape[1], 256):
            spread(nn(d[row : row + block], x[:, j : j + 256]), 0, j // 128, src)
        if k == 0:
            load.wait()
        for i in range(block):
            to = row_at[0, row + i] * PITCH
            for h in (0, 8):
                out[pl.ds(to + h, 8), :] = src[pl.ds(i * PITCH + h, 8), :]


def near_rows(first, size, order, diag, ordered, sofar):
    rows, depth = diag.shape
    cols = ordered.shape[1]
    block = size if size <= 512 else size // 2
    return call(
        functools.partial(near_kernel, first, size),
        f"near_{first}",
        pltpu.VMEM((rows * PITCH, 128), F32),
        tuple(map(pin, (order, diag, ordered, sofar))),
        flops=2 * size * depth * cols,
        limit=6 + block // 64,
        scratch=[pltpu.VMEM((block * PITCH, 128), F32)] * 2
        + [pltpu.SMEM(order.shape, jnp.int32), pltpu.SemaphoreType.DMA],
        specs=[VMEM] * 4,
        alias={3: 0},
    )


def quad_up_kernel(table, u0, u1, u2, u3, inner, mid, p0, p1, p2, p3, leaf, top):
    x, z, outer = place()
    quad = outer * RING + z
    size = p0.shape[0]
    for s, ref in enumerate((u0, u1, u2, u3)):
        leaf[(x - s) & 3] = ref[...]
    for k in range(2):
        up = leaf[2 * k].astype(F32) + leaf[2 * k + 1].astype(F32)
        mid[k] = masked(up, limit_of(table, 63 + 2 * quad + k))
    up = nn(mid[0], inner[2 * z, 0]) + nn(mid[1], inner[2 * z + 1, 0])
    top[...] = masked(up, limit_of(table, 31 + quad))
    for t, ref in enumerate((p0, p1, p2, p3)):
        ref[...] = top[pl.ds(pl.multiple_of(((z + t) & 3) * size, size), size), :]


def quad_up(table, pieces, inner):
    cols, width = pieces[0].shape
    return call(
        quad_up_kernel,
        "quad_up",
        (held(2, cols, width),) + (held(cols // RING, width),) * 4,
        (pin(table), *map(pin, pieces), pin(inner)),
        scratch=[pltpu.VMEM((4, cols, width), BF), pltpu.VMEM((cols, width), BF)],
    )


def group_up_kernel(table, q0, q1, q2, q3, inner, out2, out3, lift):
    x, z, group = place()
    for t, ref in enumerate((q0, q1, q2, q3)):
        out2[(z - t) & 3] = ref[...]
    for k in range(2):
        up = nn(out2[2 * k], inner[8 + 2 * k, 0]) + nn(out2[2 * k + 1], inner[9 + 2 * k, 0])
        out3[k] = masked(up, limit_of(table, 15 + 2 * group + k))
    up = nn(out3[0], inner[12, 0]) + nn(out3[1], inner[13, 0])
    four = masked(up, limit_of(table, 7 + group))
    lift[0] = four.astype(F32)
    lift[1] = nn(four, inner[14, 0])


def group_up(table, pieces, inner):
    part, width = pieces[0].shape
    return call(
        group_up_kernel,
        "group_up",
        (
            held(4, part, width),
            held(2, part, width),
            pltpu.VMEM((2, part, width), F32),
        ),
        (pin(table), *map(pin, pieces), pin(inner)),
    )


def five_kernel(table, own, peer, out):
    out[...] = masked(own[1] + peer[1], limit_of(table, 3 + (place()[2] >> 1)))


def five_up(table, own, peer):
    return call(five_kernel, "five", held(*own.shape[1:]), (pin(table), pin(own), pin(peer)))


def top_kernel(
    table, y0, y1, y2, y3, peer4, c2, c3, inner, outer, root, p0, p1, p2, p3, five, far2
):
    x, z, group = place()
    y = group >> 1
    half = y >> 1
    for s, ref in enumerate((y0, y1, y2, y3)):
        five[y ^ s] = ref[...]
    six = []
    for k in range(2):
        up = nn(five[2 * k], outer[2 * k, 0]) + nn(five[2 * k + 1], outer[2 * k + 1, 0])
        six.append(masked(up, limit_of(table, 1 + k)))
    up = nn(six[0], outer[4, 0]) + nn(six[1], outer[5, 0])
    seven = masked(up, limit_of(table, 0))
    far = masked(nt(seven, root[...]), limit_of(table, 0))
    sib = jnp.where(half == 0, six[1].astype(F32), six[0].astype(F32)).astype(BF)
    far = masked(nt(sib, outer[4 + half, 1]) + nt(far, outer[4 + half, 0]), limit_of(table, 1 + half))
    far = masked(nt(five[y ^ 1], outer[y, 1]) + nt(far, outer[y, 0]), limit_of(table, 3 + y))
    far = masked(nt(peer4[0].astype(BF), inner[14, 1]) + nt(far, inner[14, 0]), limit_of(table, 7 + group))
    for k in range(2):
        down = nt(c3[1 - k], inner[12 + k, 1]) + nt(far, inner[12 + k, 0])
        far3 = masked(down, limit_of(table, 15 + 2 * group + k))
        for i in (2 * k, 2 * k + 1):
            down = nt(c2[i ^ 1], inner[8 + i, 1]) + nt(far3, inner[8 + i, 0])
            far2[i] = masked(down, limit_of(table, 31 + 4 * group + i))
    for t, ref in enumerate((p0, p1, p2, p3)):
        ref[...] = far2[(z + t) & 3]


def top_sweep(table, fives, peer4, c2, c3, inner, outer, root):
    part, width = fives[0].shape
    return call(
        top_kernel,
        "top",
        (held(part, width),) * 4,
        (pin(table), *map(pin, (*fives, peer4, c2, c3, inner, outer, root))),
        scratch=[pltpu.VMEM((4, part, width), BF)] * 2,
    )


def quad_down_kernel(table, f0, f1, f2, f3, mid, inner, p0, p1, p2, p3, far2, far1):
    x, z, outer = place()
    quad = outer * RING + z
    size = f0.shape[0]
    for t, ref in enumerate((f0, f1, f2, f3)):
        far2[pl.ds(pl.multiple_of(((z - t) & 3) * size, size), size), :] = ref[...]
    for k in range(2):
        down = nt(mid[1 - k], inner[2 * z + k, 1]) + nt(far2[...], inner[2 * z + k, 0])
        far1[k] = masked(down, limit_of(table, 63 + 2 * quad + k))
    for s, ref in enumerate((p0, p1, p2, p3)):
        ref[...] = far1[((x + s) & 3) >> 1]


def quad_down(table, fars, mid, inner):
    part, width = fars[0].shape
    cols = part * RING
    return call(
        quad_down_kernel,
        "quad_down",
        (held(cols, width),) * 4,
        (pin(table), *map(pin, (*fars, mid, inner))),
        scratch=[pltpu.VMEM((cols, width), BF), pltpu.VMEM((2, cols, width), BF)],
    )


TAIL = 512


def tail_kernel(shifts, table, basis, sibling, node, near, *refs):
    fars = refs[: len(shifts)]
    o_hbm, buf, sem = refs[-3:]
    x, z, outer = place()
    cols = fars[0].shape[0]
    limit = limit_of(table, 127 + outer * 16 + z * RING + x)
    copies = []
    for i, (shift, far1) in enumerate(zip(shifts, fars)):
        part = (x - shift) & 3
        at = pl.ds(pl.multiple_of(part * cols, cols), cols)
        tiles = cols // 128
        down = nt(sibling[at, :], node[1]) + nt(far1[...], node[0])
        far = masked(down, limit)
        for row in range(0, basis.shape[0], TAIL):
            add = nt(basis[row : row + TAIL], far)
            value = gathered(row, TAIL, part * tiles, tiles, near) + add
            buf[i, row : row + TAIL] = value.astype(BF)
            copy = pltpu.make_async_copy(
                buf.at[i, pl.ds(row, TAIL)], o_hbm.at[pl.ds(row, TAIL), at], sem.at[len(copies)]
            )
            copy.start()
            copies.append(copy)
    for copy in copies:
        copy.wait()


def add_far(shifts, table, basis, sibling, node, near, fars, sofar):
    rows, width = basis.shape
    cols = fars[0].shape[0]
    args = [pin(a) for a in (table, basis, sibling, node, near, *fars)]
    specs = [VMEM] * len(args)
    alias = {}
    if sofar is not None:
        alias = {len(args): 0}
        args.append(sofar)
        specs.append(HBM)
    return pl.pallas_call(
        functools.partial(tail_kernel, shifts),
        out_shape=sds(rows, cols * RING),
        in_specs=specs,
        out_specs=HBM,
        input_output_aliases=alias,
        scratch_shapes=[
            pltpu.VMEM((len(shifts), rows, cols), BF),
            pltpu.SemaphoreType.DMA((len(shifts) * rows // TAIL,)),
        ],
        compiler_params=params(14 * 2**20),
        cost_estimate=cost(2 * rows * width * cols, 3 * 2**20),
        name="tail_" + "".join(map(str, shifts)),
    )(*args)


def ring_x(block, shift):
    route = [(z * RING + x, z * RING + (x + shift) % RING) for z in range(RING) for x in range(RING)]
    return lax.ppermute(block, "inner", route)


def ring_z(block, shift):
    route = [(z * RING + x, (z + shift) % RING * RING + x) for z in range(RING) for x in range(RING)]
    return lax.ppermute(block, "inner", route)


def swap_inner(block, bits):
    return lax.ppermute(block, "inner", [(i, i ^ bits) for i in range(RING * RING)])


def swap_outer(block, bits):
    return lax.ppermute(block, "outer", [(o, o ^ bits) for o in range(2 * RING)])


def exchange(move, pieces, order=(2, 1, 3)):
    got = {0: pieces[0]}
    for s in order:
        got[s] = move(pieces[s], s)
    return [got[s] for s in range(RING)]


def body(
    points,
    leaf_order,
    diag_blocks,
    leaf_basis,
    leaf_nodes,
    inner_nodes,
    outer_nodes,
    root_coupling,
    node_ranks,
):
    inner = inner_nodes[0]
    node = leaf_nodes[0]

    basis, basis_t, x, c2, piece, limit = front(leaf_order, node_ranks, leaf_basis[0], points, node)
    c1, c3, *others = coef_rest(limit, basis_t, x, node)
    sent = {2: ring_x(piece, 2), 1: ring_x(others[0], 1), 3: ring_x(others[1], 3)}
    coefs = (c1, c2, c3)
    coef, ordered, diag, own, near, table = move(
        limit, node_ranks, leaf_order, basis_t, node, coefs, x, diag_blocks[0]
    )
    near = near_rows(0, 256, leaf_order, diag, ordered, near)
    pieces = [own, sent[1], sent[2], sent[3]]
    *pieces, coef, near = lax.optimization_barrier((*pieces, coef, near))

    mid, *parts = quad_up(table, pieces, inner)
    coef, *parts = lax.optimization_barrier((coef, *parts))
    parts = exchange(ring_z, parts)
    sibling = swap_inner(coef, 1)
    near = near_rows(256, 256, leaf_order, diag, ordered, near)
    *parts, near = lax.optimization_barrier((*parts, near))
    c2, c3, lift = group_up(table, parts, inner)
    peer = swap_outer(lift, 1)
    near = near_rows(512, 128, leaf_order, diag, ordered, near)
    peer, near = lax.optimization_barrier((peer, near))
    five = five_up(table, lift, peer)
    fives = [five] + [swap_outer(five, 2 * s) for s in (1, 2, 3)]
    near = near_rows(640, 256, leaf_order, diag, ordered, near)
    *fives, near = lax.optimization_barrier((*fives, near))
    parts = top_sweep(table, fives, peer, c2, c3, inner, outer_nodes, root_coupling)
    parts = exchange(ring_z, parts)
    near = near_rows(896, 256, leaf_order, diag, ordered, near)
    *parts, near, sibling = lax.optimization_barrier((*parts, near, sibling))
    fars = quad_down(table, parts, mid, inner)
    fars = exchange(ring_x, fars)
    near = near_rows(1152, 896, leaf_order, diag, ordered, near)
    add = functools.partial(add_far, table=table, basis=basis, sibling=sibling, node=node, near=near)
    return add((0, 1, 3, 2), fars=[fars[s] for s in (0, 1, 3, 2)], sofar=None)


def solution(mesh):
    in_specs = (
        P(("outer", "inner"), None),
        P(("outer", "inner"), None),
        P(("outer", "inner"), None, None),
        P(("outer", "inner"), None, None),
        P(("outer", "inner"), None, None, None),
        P("outer", None, None, None, None),
        P(),
        P(),
        P(),
    )
    out_specs = P(("outer", "inner"), None)
    return jax.shard_map(body, mesh=mesh, in_specs=in_specs, out_specs=out_specs, check_vma=False)
```

```python
import functools

import jax
import jax.numpy as jnp
from jax import lax
from jax.experimental import pallas as pl
from jax.experimental.pallas import tpu as pltpu
from jax.sharding import PartitionSpec as P

BF = jnp.bfloat16
F32 = jnp.float32
RING = 4
SMALL = 24 * 2**20


def nn(a, b):
    return jnp.dot(a, b, preferred_element_type=F32)


def nt(a, b):
    return lax.dot_general(a, b, (((1,), (1,)), ((), ())), preferred_element_type=F32)


def masked(value, limit):
    lane = lax.broadcasted_iota(jnp.int32, value.shape, 1)
    return jnp.where(lane < limit, value, 0.0).astype(BF)


def limit_of(table, heap_id):
    return table[pl.ds(heap_id, 1), :]


def params(limit):
    return pltpu.CompilerParams(vmem_limit_bytes=limit)


def cost(flops, moved):
    return pl.CostEstimate(flops=flops, bytes_accessed=moved, transcendentals=0)


def sds(*shape):
    return jax.ShapeDtypeStruct(shape, BF)


def held(*shape):
    return pltpu.VMEM(shape, BF)


def pin(x, space=pltpu.VMEM):
    return pltpu.with_memory_space_constraint(x, space)


VMEM = pl.BlockSpec(memory_space=pltpu.VMEM)
HBM = pl.BlockSpec(memory_space=pltpu.HBM)


def place():
    inner = lax.axis_index("inner")
    return inner & 3, inner >> 2, lax.axis_index("outer")


def call(kernel, name, out_shapes, args, flops=2**28, limit=5, scratch=(), specs=None, alias={}):
    many = isinstance(out_shapes, tuple)
    return pl.pallas_call(
        kernel,
        out_shape=out_shapes,
        in_specs=specs or [VMEM] * len(args),
        out_specs=(VMEM,) * len(out_shapes) if many else VMEM,
        input_output_aliases=alias,
        scratch_shapes=list(scratch),
        compiler_params=params(limit * 2**20),
        cost_estimate=cost(flops, 2**20),
        name=name,
    )(*args)


def shuffle_basis(order, basis, out, out_t, src, dst):
    rows = basis.shape[0]

    @pl.loop(0, rows // 64)
    def _(i):
        for j in range(64):
            to = order[0, i * 64 + j] * 3
            dst[pl.ds(to, 2), :] = src[pl.ds(i * 192 + j * 3, 2), :]

    @pl.loop(0, rows // 256)
    def _(b):
        for t in range(2):
            parts = []
            for r in range(32):
                base = (b * 256 + r * 8) * 3 + t
                parts.append(dst[pl.ds(base, 8, stride=3), :])
            x = jnp.concatenate(parts, axis=0)
            start = pl.multiple_of(b * 256, 256)
            out[pl.ds(start, 256), t * 128 : (t + 1) * 128] = x.astype(BF)
            out_t[t * 128 : (t + 1) * 128, pl.ds(start, 256)] = x.T.astype(BF)


def spread_basis(first, rows, basis, src):
    @pl.loop(first // 64, (first + rows) // 64)
    def _(b):
        for r in range(4):
            for t in range(2):
                start = pl.multiple_of(b * 64 + r * 16, 16)
                x = basis[pl.ds(start, 16), t * 128 : (t + 1) * 128].astype(F32)
                base = (b * 64 + r * 16) * 3 + t
                src[pl.ds(base, 8, stride=3), :] = x[:8]
                src[pl.ds(base + 24, 8, stride=3), :] = x[8:]


def coef_product(shift, basis_t, x):
    cols = x.shape[1] // RING
    start = pl.multiple_of(((place()[0] + shift) & 3) * cols, cols)
    return nn(basis_t[...], x[:, pl.ds(start, cols)])


def coef_finish(product, limit, transfer, coef, piece):
    c = masked(product.T, limit[0:1])
    coef[...] = c
    piece[...] = nn(c, transfer[...]).astype(BF)


def front_kernel(
    order_hbm, ranks_hbm, basis_hbm, x_hbm, node_hbm,
    out, out_t, x, coef, piece, limit, transfer,
    order, ranks, basis, src, dst, sem,
):
    cols = piece.shape[0]
    ring, z, outer = place()

    def fetch(k):
        start = pl.multiple_of(lax.rem(ring + (2, 1, 3, 0)[k], RING) * cols, cols)
        part = pl.ds(start, cols)
        return pltpu.make_async_copy(x_hbm.at[:, part], x.at[:, part], sem.at[k])

    size = basis.shape[0] // 4
    parts = []
    for k in range(4):
        part = pl.ds(k * size, size)
        parts.append(pltpu.make_async_copy(basis_hbm.at[part], basis.at[part], sem.at[7 + k]))
        parts[k].start()
    loads = [
        pltpu.make_async_copy(order_hbm, order, sem.at[4]),
        pltpu.make_async_copy(ranks_hbm, ranks, sem.at[5]),
        pltpu.make_async_copy(node_hbm.at[0], transfer, sem.at[6]),
    ]
    for load in loads:
        load.start()
    for k in range(RING):
        fetch(k).start()
    for k in range(4):
        parts[k].wait()
        spread_basis(k * size, size, basis, src)
    for load in loads:
        load.wait()
    limit[...] = jnp.full(limit.shape, ranks[127 + outer * 16 + z * RING + ring], jnp.int32)
    shuffle_basis(order, basis, out, out_t, src, dst)
    fetch(0).wait()
    coef_finish(coef_product(2, out_t, x), limit, transfer, coef, piece)
    for k in range(1, RING):
        fetch(k).wait()


def front(order, ranks, basis, points, nodes):
    rows, width = basis.shape
    cols = points.shape[1]
    return call(
        front_kernel,
        "front",
        (
            held(rows, width),
            held(width, rows),
            held(rows, cols),
            held(cols // RING, width),
            held(cols // RING, width),
            pltpu.VMEM((8, width), jnp.int32),
            held(width, width),
        ),
        [pin(a, pltpu.HBM) for a in (order, ranks, basis, points, nodes)],
        flops=2**31,
        limit=13,
        scratch=[
            pltpu.SMEM(order.shape, jnp.int32),
            pltpu.SMEM(ranks.shape, jnp.int32),
            pltpu.VMEM((rows, width), BF),
            pltpu.VMEM((rows * 3, 128), F32),
            pltpu.VMEM((rows * 3, 128), F32),
            pltpu.SemaphoreType.DMA((11,)),
        ],
        specs=[HBM] * 5,
    )


def coef_kernel(limit, basis_t, x, transfer, c1, c3, p1, p3):
    product1 = coef_product(1, basis_t, x)
    product3 = coef_product(3, basis_t, x)
    coef_finish(product1, limit, transfer, c1, p1)
    coef_finish(product3, limit, transfer, c3, p3)


def coef_rest(limit, basis_t, x, transfer):
    return call(
        coef_kernel,
        "coef",
        (held(x.shape[1] // RING, basis_t.shape[0]),) * 4,
        tuple(map(pin, (limit, basis_t, x, transfer))),
        flops=2**30,
    )


PITCH = 17
GROUP = 64


def spread(value, first_row, first_tile, to):
    for r in range(0, value.shape[0], 8):
        for t in range(value.shape[1] // 128):
            at = (first_row + r) * PITCH + first_tile + t
            to[pl.ds(at, 8, stride=PITCH), :] = value[r : r + 8, t * 128 : (t + 1) * 128]


def gathered(first_row, rows, first_tile, tiles, of):
    columns = []
    for t in range(tiles):
        parts = []
        for r in range(0, rows, 8):
            at = (first_row + r) * PITCH + first_tile + t
            parts.append(of[pl.ds(at, 8, stride=PITCH), :])
        columns.append(jnp.concatenate(parts, axis=0))
    return jnp.concatenate(columns, axis=1)


def move_rows(row_at, x, src, dst):
    rows = x.shape[0]
    tiles = x.shape[1] // 128

    @pl.loop(0, rows // 32)
    def _(b):
        for r in range(0, 32, 16):
            start = pl.multiple_of(b * 32 + r, 16)
            for t in range(tiles):
                v = x[pl.ds(start, 16), t * 128 : (t + 1) * 128].astype(F32)
                spread(v, b * 32 + r, t, src)

    @pl.loop(0, rows // (2 * GROUP))
    def _(i):
        first = pl.multiple_of(i * (2 * GROUP), 2 * GROUP)
        for g in range(2):
            for j in range(GROUP):
                s = row_at[0, first + g * GROUP + j]
                for h in range(0, tiles, 8):
                    dst[g][pl.ds(j * PITCH + h, 8), :] = src[pl.ds(s + h, 8), :]
        for g in range(2):
            for r in range(0, GROUP, 16):
                for t in range(tiles):
                    v = gathered(r, 16, t, 1, dst[g]).astype(BF)
                    x[pl.ds(first + g * GROUP + r, 16), t * 128 : (t + 1) * 128] = v


def move_kernel(
    limit, order, basis_t, transfer, c1, c2, c3, x_in, diag_hbm, ranks_hbm,
    coef, x, diag, piece, src, table, scaled,
    even, odd, row_at, ranks, sem,
):
    size = diag.shape[0] // 4
    loads = []
    for k in range(4):
        part = pl.ds(k * size, size)
        loads.append(pltpu.make_async_copy(diag_hbm.at[part], diag.at[part], sem.at[k]))
        loads[k].start()
    scaled[...] = order[...] * PITCH
    load = pltpu.make_async_copy(scaled, row_at, sem.at[4])
    load.start()
    load_ranks = pltpu.make_async_copy(ranks_hbm, ranks, sem.at[5])
    load_ranks.start()
    cols = piece.shape[0]
    ring = place()[0]

    def rows_of(shift):
        return coef.at[pl.ds(pl.multiple_of(((ring + shift) & 3) * cols, cols), cols)]

    coef_finish(coef_product(0, basis_t, x), limit, transfer, rows_of(0), piece)
    for shift, ref in ((1, c1), (2, c2), (3, c3)):
        rows_of(shift)[...] = ref[...]
    load_ranks.wait()
    z, outer = place()[1:]
    quad = outer * RING + z
    used = [0, 1, 2, 3 + (outer >> 1), 7 + outer, 15 + 2 * outer, 16 + 2 * outer]
    used += [31 + RING * outer + k for k in range(RING)]
    used += [63 + 2 * quad, 64 + 2 * quad, 127 + RING * quad + ring]
    for node_id in used:
        table[pl.ds(node_id, 1), :] = jnp.full((1, table.shape[1]), ranks[node_id], jnp.int32)
    load.wait()
    move_rows(row_at, x, src, (even, odd))
    for load in loads:
        load.wait()


def move(limit, ranks, order, basis_t, transfer, coefs, x, diag):
    rows, cols = x.shape
    width = basis_t.shape[0]
    return call(
        move_kernel,
        "move",
        (
            held(cols, width),
            held(rows, cols),
            held(rows, cols),
            held(cols // RING, width),
            pltpu.VMEM((rows * PITCH, 128), F32),
            pltpu.VMEM((ranks.shape[0] + 1, width), jnp.int32),
            pltpu.VMEM(order.shape, jnp.int32),
        ),
        (
            *map(pin, (limit, order, basis_t, transfer, *coefs, x)),
            pin(diag, pltpu.HBM),
            pin(ranks, pltpu.HBM),
        ),
        flops=2**33,
        limit=6,
        scratch=[
            pltpu.VMEM((GROUP * PITCH, 128), F32),
            pltpu.VMEM((GROUP * PITCH, 128), F32),
            pltpu.SMEM(order.shape, jnp.int32),
            pltpu.SMEM(ranks.shape, jnp.int32),
            pltpu.SemaphoreType.DMA((6,)),
        ],
        specs=[VMEM] * 8 + [HBM] * 2,
        alias={7: 1},
    )


def near_kernel(first, size, order, d, x, near_in, out, even, odd, row_at, sem):
    block = even.shape[0] // PITCH
    load = pltpu.make_async_copy(order, row_at, sem)
    load.start()
    for k, row in enumerate(range(first, first + size, block)):
        src = (even, odd)[k % 2]
        for j in range(0, x.shape[1], 256):
            spread(nn(d[row : row + block], x[:, j : j + 256]), 0, j // 128, src)
        if k == 0:
            load.wait()
        for i in range(block):
            to = row_at[0, row + i]
            for h in (0, 8):
                out[pl.ds(to + h, 8), :] = src[pl.ds(i * PITCH + h, 8), :]


def near_rows(first, size, order, diag, ordered, sofar):
    rows, depth = diag.shape
    cols = ordered.shape[1]
    block = size if size <= 512 else size // 2
    return call(
        functools.partial(near_kernel, first, size),
        f"near_{first}",
        pltpu.VMEM((rows * PITCH, 128), F32),
        tuple(map(pin, (order, diag, ordered, sofar))),
        flops=2 * size * depth * cols,
        limit=6 + block // 64,
        scratch=[pltpu.VMEM((block * PITCH, 128), F32)] * 2
        + [pltpu.SMEM(order.shape, jnp.int32), pltpu.SemaphoreType.DMA],
        specs=[VMEM] * 4,
        alias={3: 0},
    )


def quad_up_kernel(table, u0, u1, u2, u3, inner, mid, p0, p1, p2, p3, leaf, top):
    x, z, outer = place()
    quad = outer * RING + z
    size = p0.shape[0]
    for s, ref in enumerate((u0, u1, u2, u3)):
        leaf[(x - s) & 3] = ref[...]
    for k in range(2):
        up = leaf[2 * k].astype(F32) + leaf[2 * k + 1].astype(F32)
        mid[k] = masked(up, limit_of(table, 63 + 2 * quad + k))
    up = nn(mid[0], inner[2 * z, 0]) + nn(mid[1], inner[2 * z + 1, 0])
    top[...] = masked(up, limit_of(table, 31 + quad))
    for t, ref in enumerate((p0, p1, p2, p3)):
        ref[...] = top[pl.ds(pl.multiple_of(((z + t) & 3) * size, size), size), :]


def quad_up(table, pieces, inner):
    cols, width = pieces[0].shape
    return call(
        quad_up_kernel,
        "quad_up",
        (held(2, cols, width),) + (held(cols // RING, width),) * 4,
        (pin(table), *map(pin, pieces), pin(inner)),
        scratch=[pltpu.VMEM((4, cols, width), BF), pltpu.VMEM((cols, width), BF)],
    )


def group_up_kernel(table, q0, q1, q2, q3, inner, out2, out3, lift):
    x, z, group = place()
    for t, ref in enumerate((q0, q1, q2, q3)):
        out2[(z - t) & 3] = ref[...]
    for k in range(2):
        up = nn(out2[2 * k], inner[8 + 2 * k, 0]) + nn(out2[2 * k + 1], inner[9 + 2 * k, 0])
        out3[k] = masked(up, limit_of(table, 15 + 2 * group + k))
    up = nn(out3[0], inner[12, 0]) + nn(out3[1], inner[13, 0])
    four = masked(up, limit_of(table, 7 + group))
    lift[0] = four.astype(F32)
    lift[1] = nn(four, inner[14, 0])


def group_up(table, pieces, inner):
    part, width = pieces[0].shape
    return call(
        group_up_kernel,
        "group_up",
        (
            held(4, part, width),
            held(2, part, width),
            pltpu.VMEM((2, part, width), F32),
        ),
        (pin(table), *map(pin, pieces), pin(inner)),
    )


def five_kernel(table, own, peer, out):
    out[...] = masked(own[1] + peer[1], limit_of(table, 3 + (place()[2] >> 1)))


def five_up(table, own, peer):
    return call(five_kernel, "five", held(*own.shape[1:]), (pin(table), pin(own), pin(peer)))


def top_kernel(
    table, y0, y1, y2, y3, peer4, c2, c3, inner, outer, root, p0, p1, p2, p3, five, far2
):
    x, z, group = place()
    y = group >> 1
    half = y >> 1
    for s, ref in enumerate((y0, y1, y2, y3)):
        five[y ^ s] = ref[...]
    six = []
    for k in range(2):
        up = nn(five[2 * k], outer[2 * k, 0]) + nn(five[2 * k + 1], outer[2 * k + 1, 0])
        six.append(masked(up, limit_of(table, 1 + k)))
    up = nn(six[0], outer[4, 0]) + nn(six[1], outer[5, 0])
    seven = masked(up, limit_of(table, 0))
    far = masked(nt(seven, root[...]), limit_of(table, 0))
    sib = jnp.where(half == 0, six[1].astype(F32), six[0].astype(F32)).astype(BF)
    far = masked(nt(sib, outer[4 + half, 1]) + nt(far, outer[4 + half, 0]), limit_of(table, 1 + half))
    far = masked(nt(five[y ^ 1], outer[y, 1]) + nt(far, outer[y, 0]), limit_of(table, 3 + y))
    far = masked(nt(peer4[0].astype(BF), inner[14, 1]) + nt(far, inner[14, 0]), limit_of(table, 7 + group))
    for k in range(2):
        down = nt(c3[1 - k], inner[12 + k, 1]) + nt(far, inner[12 + k, 0])
        far3 = masked(down, limit_of(table, 15 + 2 * group + k))
        for i in (2 * k, 2 * k + 1):
            down = nt(c2[i ^ 1], inner[8 + i, 1]) + nt(far3, inner[8 + i, 0])
            far2[i] = masked(down, limit_of(table, 31 + 4 * group + i))
    for t, ref in enumerate((p0, p1, p2, p3)):
        ref[...] = far2[(z + t) & 3]


def top_sweep(table, fives, peer4, c2, c3, inner, outer, root):
    part, width = fives[0].shape
    return call(
        top_kernel,
        "top",
        (held(part, width),) * 4,
        (pin(table), *map(pin, (*fives, peer4, c2, c3, inner, outer, root))),
        scratch=[pltpu.VMEM((4, part, width), BF)] * 2,
    )


def quad_down_kernel(table, f0, f1, f2, f3, mid, inner, p0, p1, p2, p3, far2, far1):
    x, z, outer = place()
    quad = outer * RING + z
    size = f0.shape[0]
    for t, ref in enumerate((f0, f1, f2, f3)):
        far2[pl.ds(pl.multiple_of(((z - t) & 3) * size, size), size), :] = ref[...]
    for k in range(2):
        down = nt(mid[1 - k], inner[2 * z + k, 1]) + nt(far2[...], inner[2 * z + k, 0])
        far1[k] = masked(down, limit_of(table, 63 + 2 * quad + k))
    for s, ref in enumerate((p0, p1, p2, p3)):
        ref[...] = far1[((x + s) & 3) >> 1]


def quad_down(table, fars, mid, inner):
    part, width = fars[0].shape
    cols = part * RING
    return call(
        quad_down_kernel,
        "quad_down",
        (held(cols, width),) * 4,
        (pin(table), *map(pin, (*fars, mid, inner))),
        scratch=[pltpu.VMEM((cols, width), BF), pltpu.VMEM((2, cols, width), BF)],
    )


TAIL = 256


def tail_kernel(shifts, table, basis, sibling, node, near, *refs):
    fars = refs[: len(shifts)]
    o_hbm, buf, sem = refs[-3:]
    x, z, outer = place()
    cols = fars[0].shape[0]
    limit = limit_of(table, 127 + outer * 16 + z * RING + x)
    copies = []
    for i, (shift, far1) in enumerate(zip(shifts, fars)):
        part = (x - shift) & 3
        at = pl.ds(pl.multiple_of(part * cols, cols), cols)
        tiles = cols // 128
        down = nt(sibling[at, :], node[1]) + nt(far1[...], node[0])
        far = masked(down, limit)
        for row in range(0, basis.shape[0], TAIL):
            add = nt(basis[row : row + TAIL], far)
            value = gathered(row, TAIL, part * tiles, tiles, near) + add
            buf[i, row : row + TAIL] = value.astype(BF)
            copy = pltpu.make_async_copy(
                buf.at[i, pl.ds(row, TAIL)], o_hbm.at[pl.ds(row, TAIL), at], sem.at[len(copies)]
            )
            copy.start()
            copies.append(copy)
    for copy in copies:
        copy.wait()


def add_far(shifts, table, basis, sibling, node, near, fars, sofar):
    rows, width = basis.shape
    cols = fars[0].shape[0]
    args = [pin(a) for a in (table, basis, sibling, node, near, *fars)]
    specs = [VMEM] * len(args)
    alias = {}
    if sofar is not None:
        alias = {len(args): 0}
        args.append(sofar)
        specs.append(HBM)
    return pl.pallas_call(
        functools.partial(tail_kernel, shifts),
        out_shape=sds(rows, cols * RING),
        in_specs=specs,
        out_specs=HBM,
        input_output_aliases=alias,
        scratch_shapes=[
            pltpu.VMEM((len(shifts), rows, cols), BF),
            pltpu.SemaphoreType.DMA((len(shifts) * rows // TAIL,)),
        ],
        compiler_params=params(14 * 2**20),
        cost_estimate=cost(2 * rows * width * cols, 3 * 2**20),
        name="tail_" + "".join(map(str, shifts)),
    )(*args)


def ring_x(block, shift):
    route = [(z * RING + x, z * RING + (x + shift) % RING) for z in range(RING) for x in range(RING)]
    return lax.ppermute(block, "inner", route)


def ring_z(block, shift):
    route = [(z * RING + x, (z + shift) % RING * RING + x) for z in range(RING) for x in range(RING)]
    return lax.ppermute(block, "inner", route)


def swap_inner(block, bits):
    return lax.ppermute(block, "inner", [(i, i ^ bits) for i in range(RING * RING)])


def swap_outer(block, bits):
    return lax.ppermute(block, "outer", [(o, o ^ bits) for o in range(2 * RING)])


def exchange(move, pieces, order=(2, 1, 3)):
    got = {0: pieces[0]}
    for s in order:
        got[s] = move(pieces[s], s)
    return [got[s] for s in range(RING)]


def body(
    points,
    leaf_order,
    diag_blocks,
    leaf_basis,
    leaf_nodes,
    inner_nodes,
    outer_nodes,
    root_coupling,
    node_ranks,
):
    inner = inner_nodes[0]
    node = leaf_nodes[0]

    basis, basis_t, x, c2, piece, limit, transfer = front(
        leaf_order, node_ranks, leaf_basis[0], points, node
    )
    c1, c3, *others = coef_rest(limit, basis_t, x, transfer)
    sent = {2: ring_x(piece, 2), 1: ring_x(others[0], 1), 3: ring_x(others[1], 3)}
    coefs = (c1, c2, c3)
    coef, ordered, diag, own, near, table, row_at = move(
        limit, node_ranks, leaf_order, basis_t, transfer, coefs, x, diag_blocks[0]
    )
    near = near_rows(0, 256, row_at, diag, ordered, near)
    pieces = [own, sent[1], sent[2], sent[3]]
    *pieces, coef, near = lax.optimization_barrier((*pieces, coef, near))

    mid, *parts = quad_up(table, pieces, inner)
    coef, *parts = lax.optimization_barrier((coef, *parts))
    parts = exchange(ring_z, parts)
    sibling = swap_inner(coef, 1)
    near = near_rows(256, 256, row_at, diag, ordered, near)
    *parts, near = lax.optimization_barrier((*parts, near))
    c2, c3, lift = group_up(table, parts, inner)
    peer = swap_outer(lift, 1)
    near = near_rows(512, 128, row_at, diag, ordered, near)
    peer, near = lax.optimization_barrier((peer, near))
    five = five_up(table, lift, peer)
    fives = [five] + [swap_outer(five, 2 * s) for s in (1, 2, 3)]
    near = near_rows(640, 256, row_at, diag, ordered, near)
    *fives, near = lax.optimization_barrier((*fives, near))
    parts = top_sweep(table, fives, peer, c2, c3, inner, outer_nodes, root_coupling)
    parts = exchange(ring_z, parts)
    near = near_rows(896, 256, row_at, diag, ordered, near)
    *parts, near, sibling = lax.optimization_barrier((*parts, near, sibling))
    fars = quad_down(table, parts, mid, inner)
    fars = exchange(ring_x, fars)
    near = near_rows(1152, 896, row_at, diag, ordered, near)
    add = functools.partial(add_far, table=table, basis=basis, sibling=sibling, node=node, near=near)
    return add((0, 1, 3, 2), fars=[fars[s] for s in (0, 1, 3, 2)], sofar=None)


def solution(mesh):
    in_specs = (
        P(("outer", "inner"), None),
        P(("outer", "inner"), None),
        P(("outer", "inner"), None, None),
        P(("outer", "inner"), None, None),
        P(("outer", "inner"), None, None, None),
        P("outer", None, None, None, None),
        P(),
        P(),
        P(),
    )
    out_specs = P(("outer", "inner"), None)
    return jax.shard_map(body, mesh=mesh, in_specs=in_specs, out_specs=out_specs, check_vma=False)
```

```python
import functools

import jax
import jax.numpy as jnp
from jax import lax
from jax.experimental import pallas as pl
from jax.experimental.pallas import tpu as pltpu
from jax.sharding import PartitionSpec as P

BF = jnp.bfloat16
F32 = jnp.float32
RING = 4
SMALL = 24 * 2**20


def nn(a, b):
    return jnp.dot(a, b, preferred_element_type=F32)


def nt(a, b):
    return lax.dot_general(a, b, (((1,), (1,)), ((), ())), preferred_element_type=F32)


def masked(value, limit):
    lane = lax.broadcasted_iota(jnp.int32, value.shape, 1)
    return jnp.where(lane < limit, value, 0.0).astype(BF)


def limit_of(table, heap_id):
    return table[pl.ds(heap_id, 1), :]


def params(limit):
    return pltpu.CompilerParams(vmem_limit_bytes=limit)


def cost(flops, moved):
    return pl.CostEstimate(flops=flops, bytes_accessed=moved, transcendentals=0)


def sds(*shape):
    return jax.ShapeDtypeStruct(shape, BF)


def held(*shape):
    return pltpu.VMEM(shape, BF)


def pin(x, space=pltpu.VMEM):
    return pltpu.with_memory_space_constraint(x, space)


VMEM = pl.BlockSpec(memory_space=pltpu.VMEM)
HBM = pl.BlockSpec(memory_space=pltpu.HBM)


def place():
    inner = lax.axis_index("inner")
    return inner & 3, inner >> 2, lax.axis_index("outer")


def call(kernel, name, out_shapes, args, flops=2**28, limit=5, scratch=(), specs=None, alias={}):
    many = isinstance(out_shapes, tuple)
    return pl.pallas_call(
        kernel,
        out_shape=out_shapes,
        in_specs=specs or [VMEM] * len(args),
        out_specs=(VMEM,) * len(out_shapes) if many else VMEM,
        input_output_aliases=alias,
        scratch_shapes=list(scratch),
        compiler_params=params(limit * 2**20),
        cost_estimate=cost(flops, 2**20),
        name=name,
    )(*args)


def shuffle_basis(order, basis, out, out_t, src, dst):
    rows = basis.shape[0]

    @pl.loop(0, rows // 64)
    def _(i):
        for j in range(64):
            to = order[0, i * 64 + j] * 3
            dst[pl.ds(to, 2), :] = src[pl.ds(i * 192 + j * 3, 2), :]

    @pl.loop(0, rows // 256)
    def _(b):
        for t in range(2):
            parts = []
            for r in range(32):
                base = (b * 256 + r * 8) * 3 + t
                parts.append(dst[pl.ds(base, 8, stride=3), :])
            x = jnp.concatenate(parts, axis=0)
            start = pl.multiple_of(b * 256, 256)
            out[pl.ds(start, 256), t * 128 : (t + 1) * 128] = x.astype(BF)
            out_t[t * 128 : (t + 1) * 128, pl.ds(start, 256)] = x.T.astype(BF)


def spread_basis(first, rows, basis, src):
    @pl.loop(first // 64, (first + rows) // 64)
    def _(b):
        for r in range(4):
            for t in range(2):
                start = pl.multiple_of(b * 64 + r * 16, 16)
                x = basis[pl.ds(start, 16), t * 128 : (t + 1) * 128].astype(F32)
                base = (b * 64 + r * 16) * 3 + t
                src[pl.ds(base, 8, stride=3), :] = x[:8]
                src[pl.ds(base + 24, 8, stride=3), :] = x[8:]


def coef_product(shift, basis_t, x):
    cols = x.shape[1] // RING
    start = pl.multiple_of(((place()[0] + shift) & 3) * cols, cols)
    return nn(basis_t[...], x[:, pl.ds(start, cols)])


def coef_finish(product, limit, transfer, coef, piece):
    c = masked(product.T, limit[0:1])
    coef[...] = c
    piece[...] = nn(c, transfer[...]).astype(BF)


def front_kernel(
    order_hbm, ranks_hbm, basis_hbm, x_hbm, node_hbm,
    out, out_t, x, coef, piece, limit, transfer,
    order, ranks, basis, src, dst, sem,
):
    cols = piece.shape[0]
    ring, z, outer = place()

    def fetch(k):
        start = pl.multiple_of(lax.rem(ring + (2, 1, 3, 0)[k], RING) * cols, cols)
        part = pl.ds(start, cols)
        return pltpu.make_async_copy(x_hbm.at[:, part], x.at[:, part], sem.at[k])

    size = basis.shape[0] // 4
    parts = []
    for k in range(4):
        part = pl.ds(k * size, size)
        parts.append(pltpu.make_async_copy(basis_hbm.at[part], basis.at[part], sem.at[7 + k]))
        parts[k].start()
    loads = [
        pltpu.make_async_copy(order_hbm, order, sem.at[4]),
        pltpu.make_async_copy(ranks_hbm, ranks, sem.at[5]),
        pltpu.make_async_copy(node_hbm.at[0], transfer, sem.at[6]),
    ]
    for load in loads:
        load.start()
    for k in range(RING):
        fetch(k).start()
    for k in range(4):
        parts[k].wait()
        spread_basis(k * size, size, basis, src)
    for load in loads:
        load.wait()
    limit[...] = jnp.full(limit.shape, ranks[127 + outer * 16 + z * RING + ring], jnp.int32)
    shuffle_basis(order, basis, out, out_t, src, dst)
    fetch(0).wait()
    coef_finish(coef_product(2, out_t, x), limit, transfer, coef, piece)
    for k in range(1, RING):
        fetch(k).wait()


def front(order, ranks, basis, points, nodes):
    rows, width = basis.shape
    cols = points.shape[1]
    return call(
        front_kernel,
        "front",
        (
            held(rows, width),
            held(width, rows),
            held(rows, cols),
            held(cols // RING, width),
            held(cols // RING, width),
            pltpu.VMEM((8, width), jnp.int32),
            held(width, width),
        ),
        [pin(a, pltpu.HBM) for a in (order, ranks, basis, points, nodes)],
        flops=2**31,
        limit=13,
        scratch=[
            pltpu.SMEM(order.shape, jnp.int32),
            pltpu.SMEM(ranks.shape, jnp.int32),
            pltpu.VMEM((rows, width), BF),
            pltpu.VMEM((rows * 3, 128), F32),
            pltpu.VMEM((rows * 3, 128), F32),
            pltpu.SemaphoreType.DMA((11,)),
        ],
        specs=[HBM] * 5,
    )


def coef_kernel(limit, basis_t, x, transfer, c1, c3, p1, p3):
    product1 = coef_product(1, basis_t, x)
    product3 = coef_product(3, basis_t, x)
    coef_finish(product1, limit, transfer, c1, p1)
    coef_finish(product3, limit, transfer, c3, p3)


def coef_rest(limit, basis_t, x, transfer):
    return call(
        coef_kernel,
        "coef",
        (held(x.shape[1] // RING, basis_t.shape[0]),) * 4,
        tuple(map(pin, (limit, basis_t, x, transfer))),
        flops=2**30,
    )


PITCH = 17
GROUP = 128


def spread(value, first_row, first_tile, to):
    for r in range(0, value.shape[0], 8):
        for t in range(value.shape[1] // 128):
            at = (first_row + r) * PITCH + first_tile + t
            to[pl.ds(at, 8, stride=PITCH), :] = value[r : r + 8, t * 128 : (t + 1) * 128]


def gathered(first_row, rows, first_tile, tiles, of):
    columns = []
    for t in range(tiles):
        parts = []
        for r in range(0, rows, 8):
            at = (first_row + r) * PITCH + first_tile + t
            parts.append(of[pl.ds(at, 8, stride=PITCH), :])
        columns.append(jnp.concatenate(parts, axis=0))
    return jnp.concatenate(columns, axis=1)


def move_rows(row_at, x, src, dst):
    rows = x.shape[0]
    tiles = x.shape[1] // 128

    @pl.loop(0, rows // 64)
    def _(b):
        for r in range(0, 64, 16):
            start = pl.multiple_of(b * 64 + r, 16)
            for t in range(tiles):
                v = x[pl.ds(start, 16), t * 128 : (t + 1) * 128].astype(F32)
                spread(v, b * 64 + r, t, src)

    @pl.loop(0, rows // (2 * GROUP))
    def _(i):
        first = pl.multiple_of(i * (2 * GROUP), 2 * GROUP)
        for g in range(2):
            for j in range(GROUP):
                s = row_at[0, first + g * GROUP + j]
                for h in range(0, tiles, 8):
                    dst[g][pl.ds(j * PITCH + h, 8), :] = src[pl.ds(s + h, 8), :]
        for g in range(2):
            for r in range(0, GROUP, 16):
                for t in range(tiles):
                    v = gathered(r, 16, t, 1, dst[g]).astype(BF)
                    x[pl.ds(first + g * GROUP + r, 16), t * 128 : (t + 1) * 128] = v


def move_kernel(
    limit, order, basis_t, transfer, c1, c2, c3, x_in, diag_hbm, ranks_hbm,
    coef, x, diag, piece, src, table, scaled,
    even, odd, row_at, ranks, sem,
):
    size = diag.shape[0] // 4
    loads = []
    for k in range(4):
        part = pl.ds(k * size, size)
        loads.append(pltpu.make_async_copy(diag_hbm.at[part], diag.at[part], sem.at[k]))
        loads[k].start()
    scaled[...] = order[...] * PITCH
    load = pltpu.make_async_copy(scaled, row_at, sem.at[4])
    load.start()
    load_ranks = pltpu.make_async_copy(ranks_hbm, ranks, sem.at[5])
    load_ranks.start()
    cols = piece.shape[0]
    ring = place()[0]

    def rows_of(shift):
        return coef.at[pl.ds(pl.multiple_of(((ring + shift) & 3) * cols, cols), cols)]

    coef_finish(coef_product(0, basis_t, x), limit, transfer, rows_of(0), piece)
    for shift, ref in ((1, c1), (2, c2), (3, c3)):
        rows_of(shift)[...] = ref[...]
    load_ranks.wait()
    z, outer = place()[1:]
    quad = outer * RING + z
    used = [0, 1, 2, 3 + (outer >> 1), 7 + outer, 15 + 2 * outer, 16 + 2 * outer]
    used += [31 + RING * outer + k for k in range(RING)]
    used += [63 + 2 * quad, 64 + 2 * quad, 127 + RING * quad + ring]
    for node_id in used:
        table[pl.ds(node_id, 1), :] = jnp.full((1, table.shape[1]), ranks[node_id], jnp.int32)
    load.wait()
    move_rows(row_at, x, src, (even, odd))
    for load in loads:
        load.wait()


def move(limit, ranks, order, basis_t, transfer, coefs, x, diag):
    rows, cols = x.shape
    width = basis_t.shape[0]
    return call(
        move_kernel,
        "move",
        (
            held(cols, width),
            held(rows, cols),
            held(rows, cols),
            held(cols // RING, width),
            pltpu.VMEM((rows * PITCH, 128), F32),
            pltpu.VMEM((ranks.shape[0] + 1, width), jnp.int32),
            pltpu.VMEM(order.shape, jnp.int32),
        ),
        (
            *map(pin, (limit, order, basis_t, transfer, *coefs, x)),
            pin(diag, pltpu.HBM),
            pin(ranks, pltpu.HBM),
        ),
        flops=2**33,
        limit=6,
        scratch=[
            pltpu.VMEM((GROUP * PITCH, 128), F32),
            pltpu.VMEM((GROUP * PITCH, 128), F32),
            pltpu.SMEM(order.shape, jnp.int32),
            pltpu.SMEM(ranks.shape, jnp.int32),
            pltpu.SemaphoreType.DMA((6,)),
        ],
        specs=[VMEM] * 8 + [HBM] * 2,
        alias={7: 1},
    )


def near_kernel(first, size, order, d, x, near_in, out, even, odd, row_at, sem):
    block = even.shape[0] // PITCH
    load = pltpu.make_async_copy(order, row_at, sem)
    load.start()
    for k, row in enumerate(range(first, first + size, block)):
        src = (even, odd)[k % 2]
        for j in range(0, x.shape[1], 256):
            spread(nn(d[row : row + block], x[:, j : j + 256]), 0, j // 128, src)
        if k == 0:
            load.wait()
        for i in range(block):
            to = row_at[0, row + i]
            for h in (0, 8):
                out[pl.ds(to + h, 8), :] = src[pl.ds(i * PITCH + h, 8), :]


def near_rows(first, size, order, diag, ordered, sofar):
    rows, depth = diag.shape
    cols = ordered.shape[1]
    block = size if size <= 512 else size // 2
    return call(
        functools.partial(near_kernel, first, size),
        f"near_{first}",
        pltpu.VMEM((rows * PITCH, 128), F32),
        tuple(map(pin, (order, diag, ordered, sofar))),
        flops=2 * size * depth * cols,
        limit=6 + block // 64,
        scratch=[pltpu.VMEM((block * PITCH, 128), F32)] * 2
        + [pltpu.SMEM(order.shape, jnp.int32), pltpu.SemaphoreType.DMA],
        specs=[VMEM] * 4,
        alias={3: 0},
    )


def quad_up_kernel(table, u0, u1, u2, u3, inner, mid, p0, p1, p2, p3, leaf, top):
    x, z, outer = place()
    quad = outer * RING + z
    size = p0.shape[0]
    for s, ref in enumerate((u0, u1, u2, u3)):
        leaf[(x - s) & 3] = ref[...]
    for k in range(2):
        up = leaf[2 * k].astype(F32) + leaf[2 * k + 1].astype(F32)
        mid[k] = masked(up, limit_of(table, 63 + 2 * quad + k))
    up = nn(mid[0], inner[2 * z, 0]) + nn(mid[1], inner[2 * z + 1, 0])
    top[...] = masked(up, limit_of(table, 31 + quad))
    for t, ref in enumerate((p0, p1, p2, p3)):
        ref[...] = top[pl.ds(pl.multiple_of(((z + t) & 3) * size, size), size), :]


def quad_up(table, pieces, inner):
    cols, width = pieces[0].shape
    return call(
        quad_up_kernel,
        "quad_up",
        (held(2, cols, width),) + (held(cols // RING, width),) * 4,
        (pin(table), *map(pin, pieces), pin(inner)),
        scratch=[pltpu.VMEM((4, cols, width), BF), pltpu.VMEM((cols, width), BF)],
    )


def group_up_kernel(table, q0, q1, q2, q3, inner, out2, out3, lift):
    x, z, group = place()
    for t, ref in enumerate((q0, q1, q2, q3)):
        out2[(z - t) & 3] = ref[...]
    for k in range(2):
        up = nn(out2[2 * k], inner[8 + 2 * k, 0]) + nn(out2[2 * k + 1], inner[9 + 2 * k, 0])
        out3[k] = masked(up, limit_of(table, 15 + 2 * group + k))
    up = nn(out3[0], inner[12, 0]) + nn(out3[1], inner[13, 0])
    four = masked(up, limit_of(table, 7 + group))
    lift[0] = four.astype(F32)
    lift[1] = nn(four, inner[14, 0])


def group_up(table, pieces, inner):
    part, width = pieces[0].shape
    return call(
        group_up_kernel,
        "group_up",
        (
            held(4, part, width),
            held(2, part, width),
            pltpu.VMEM((2, part, width), F32),
        ),
        (pin(table), *map(pin, pieces), pin(inner)),
    )


def five_kernel(table, own, peer, out):
    out[...] = masked(own[1] + peer[1], limit_of(table, 3 + (place()[2] >> 1)))


def five_up(table, own, peer):
    return call(five_kernel, "five", held(*own.shape[1:]), (pin(table), pin(own), pin(peer)))


def top_kernel(
    table, y0, y1, y2, y3, peer4, c2, c3, inner, outer, root, p0, p1, p2, p3, five, far2
):
    x, z, group = place()
    y = group >> 1
    half = y >> 1
    for s, ref in enumerate((y0, y1, y2, y3)):
        five[y ^ s] = ref[...]
    six = []
    for k in range(2):
        up = nn(five[2 * k], outer[2 * k, 0]) + nn(five[2 * k + 1], outer[2 * k + 1, 0])
        six.append(masked(up, limit_of(table, 1 + k)))
    up = nn(six[0], outer[4, 0]) + nn(six[1], outer[5, 0])
    seven = masked(up, limit_of(table, 0))
    far = masked(nt(seven, root[...]), limit_of(table, 0))
    sib = jnp.where(half == 0, six[1].astype(F32), six[0].astype(F32)).astype(BF)
    far = masked(nt(sib, outer[4 + half, 1]) + nt(far, outer[4 + half, 0]), limit_of(table, 1 + half))
    far = masked(nt(five[y ^ 1], outer[y, 1]) + nt(far, outer[y, 0]), limit_of(table, 3 + y))
    far = masked(nt(peer4[0].astype(BF), inner[14, 1]) + nt(far, inner[14, 0]), limit_of(table, 7 + group))
    for k in range(2):
        down = nt(c3[1 - k], inner[12 + k, 1]) + nt(far, inner[12 + k, 0])
        far3 = masked(down, limit_of(table, 15 + 2 * group + k))
        for i in (2 * k, 2 * k + 1):
            down = nt(c2[i ^ 1], inner[8 + i, 1]) + nt(far3, inner[8 + i, 0])
            far2[i] = masked(down, limit_of(table, 31 + 4 * group + i))
    for t, ref in enumerate((p0, p1, p2, p3)):
        ref[...] = far2[(z + t) & 3]


def top_sweep(table, fives, peer4, c2, c3, inner, outer, root):
    part, width = fives[0].shape
    return call(
        top_kernel,
        "top",
        (held(part, width),) * 4,
        (pin(table), *map(pin, (*fives, peer4, c2, c3, inner, outer, root))),
        scratch=[pltpu.VMEM((4, part, width), BF)] * 2,
    )


def quad_down_kernel(table, f0, f1, f2, f3, mid, inner, p0, p1, p2, p3, far2, far1):
    x, z, outer = place()
    quad = outer * RING + z
    size = f0.shape[0]
    for t, ref in enumerate((f0, f1, f2, f3)):
        far2[pl.ds(pl.multiple_of(((z - t) & 3) * size, size), size), :] = ref[...]
    for k in range(2):
        down = nt(mid[1 - k], inner[2 * z + k, 1]) + nt(far2[...], inner[2 * z + k, 0])
        far1[k] = masked(down, limit_of(table, 63 + 2 * quad + k))
    for s, ref in enumerate((p0, p1, p2, p3)):
        ref[...] = far1[((x + s) & 3) >> 1]


def quad_down(table, fars, mid, inner):
    part, width = fars[0].shape
    cols = part * RING
    return call(
        quad_down_kernel,
        "quad_down",
        (held(cols, width),) * 4,
        (pin(table), *map(pin, (*fars, mid, inner))),
        scratch=[pltpu.VMEM((cols, width), BF), pltpu.VMEM((2, cols, width), BF)],
    )


TAIL = 512


def tail_kernel(shifts, table, basis, sibling, node, near, *refs):
    fars = refs[: len(shifts)]
    o_hbm, buf, sem = refs[-3:]
    x, z, outer = place()
    cols = fars[0].shape[0]
    limit = limit_of(table, 127 + outer * 16 + z * RING + x)
    copies = []
    for i, (shift, far1) in enumerate(zip(shifts, fars)):
        part = (x - shift) & 3
        at = pl.ds(pl.multiple_of(part * cols, cols), cols)
        tiles = cols // 128
        down = nt(sibling[at, :], node[1]) + nt(far1[...], node[0])
        far = masked(down, limit)
        for row in range(0, basis.shape[0], TAIL):
            add = nt(basis[row : row + TAIL], far)
            value = gathered(row, TAIL, part * tiles, tiles, near) + add
            buf[i, row : row + TAIL] = value.astype(BF)
            copy = pltpu.make_async_copy(
                buf.at[i, pl.ds(row, TAIL)], o_hbm.at[pl.ds(row, TAIL), at], sem.at[len(copies)]
            )
            copy.start()
            copies.append(copy)
    for copy in copies:
        copy.wait()


def add_far(shifts, table, basis, sibling, node, near, fars, sofar):
    rows, width = basis.shape
    cols = fars[0].shape[0]
    args = [pin(a) for a in (table, basis, sibling, node, near, *fars)]
    specs = [VMEM] * len(args)
    alias = {}
    if sofar is not None:
        alias = {len(args): 0}
        args.append(sofar)
        specs.append(HBM)
    return pl.pallas_call(
        functools.partial(tail_kernel, shifts),
        out_shape=sds(rows, cols * RING),
        in_specs=specs,
        out_specs=HBM,
        input_output_aliases=alias,
        scratch_shapes=[
            pltpu.VMEM((len(shifts), rows, cols), BF),
            pltpu.SemaphoreType.DMA((len(shifts) * rows // TAIL,)),
        ],
        compiler_params=params(14 * 2**20),
        cost_estimate=cost(2 * rows * width * cols, 3 * 2**20),
        name="tail_" + "".join(map(str, shifts)),
    )(*args)


def ring_x(block, shift):
    route = [(z * RING + x, z * RING + (x + shift) % RING) for z in range(RING) for x in range(RING)]
    return lax.ppermute(block, "inner", route)


def ring_z(block, shift):
    route = [(z * RING + x, (z + shift) % RING * RING + x) for z in range(RING) for x in range(RING)]
    return lax.ppermute(block, "inner", route)


def swap_inner(block, bits):
    return lax.ppermute(block, "inner", [(i, i ^ bits) for i in range(RING * RING)])


def swap_outer(block, bits):
    return lax.ppermute(block, "outer", [(o, o ^ bits) for o in range(2 * RING)])


def exchange(move, pieces, order=(2, 1, 3)):
    got = {0: pieces[0]}
    for s in order:
        got[s] = move(pieces[s], s)
    return [got[s] for s in range(RING)]


def body(
    points,
    leaf_order,
    diag_blocks,
    leaf_basis,
    leaf_nodes,
    inner_nodes,
    outer_nodes,
    root_coupling,
    node_ranks,
):
    inner = inner_nodes[0]
    node = leaf_nodes[0]

    basis, basis_t, x, c2, piece, limit, transfer = front(
        leaf_order, node_ranks, leaf_basis[0], points, node
    )
    c1, c3, *others = coef_rest(limit, basis_t, x, transfer)
    sent = {2: ring_x(piece, 2), 1: ring_x(others[0], 1), 3: ring_x(others[1], 3)}
    coefs = (c1, c2, c3)
    coef, ordered, diag, own, near, table, row_at = move(
        limit, node_ranks, leaf_order, basis_t, transfer, coefs, x, diag_blocks[0]
    )
    near = near_rows(0, 256, row_at, diag, ordered, near)
    pieces = [own, sent[1], sent[2], sent[3]]
    *pieces, coef, near = lax.optimization_barrier((*pieces, coef, near))

    mid, *parts = quad_up(table, pieces, inner)
    coef, *parts = lax.optimization_barrier((coef, *parts))
    parts = exchange(ring_z, parts)
    sibling = swap_inner(coef, 1)
    near = near_rows(256, 256, row_at, diag, ordered, near)
    *parts, near = lax.optimization_barrier((*parts, near))
    c2, c3, lift = group_up(table, parts, inner)
    peer = swap_outer(lift, 1)
    near = near_rows(512, 128, row_at, diag, ordered, near)
    peer, near = lax.optimization_barrier((peer, near))
    five = five_up(table, lift, peer)
    fives = [five] + [swap_outer(five, 2 * s) for s in (1, 2, 3)]
    near = near_rows(640, 256, row_at, diag, ordered, near)
    *fives, near = lax.optimization_barrier((*fives, near))
    parts = top_sweep(table, fives, peer, c2, c3, inner, outer_nodes, root_coupling)
    parts = exchange(ring_z, parts)
    near = near_rows(896, 256, row_at, diag, ordered, near)
    *parts, near, sibling = lax.optimization_barrier((*parts, near, sibling))
    fars = quad_down(table, parts, mid, inner)
    fars = exchange(ring_x, fars)
    near = near_rows(1152, 896, row_at, diag, ordered, near)
    add = functools.partial(add_far, table=table, basis=basis, sibling=sibling, node=node, near=near)
    return add((0, 1, 3, 2), fars=[fars[s] for s in (0, 1, 3, 2)], sofar=None)


def solution(mesh):
    in_specs = (
        P(("outer", "inner"), None),
        P(("outer", "inner"), None),
        P(("outer", "inner"), None, None),
        P(("outer", "inner"), None, None),
        P(("outer", "inner"), None, None, None),
        P("outer", None, None, None, None),
        P(),
        P(),
        P(),
    )
    out_specs = P(("outer", "inner"), None)
    return jax.shard_map(body, mesh=mesh, in_specs=in_specs, out_specs=out_specs, check_vma=False)
```
